32 devices in a mesh: chrom: 2 (over x), samp: 16 (over z, y, core).
Axes of the slice: x: 2, y: 2, z: 4, core: 2. Of those that a mesh axis runs over, the one named last changes fastest.
Arguments:
- genotypes: int32 [6144, 6144], P('samp', 'chrom'), may hold values from 0 to 2, as said below
- frequency: float32 [6144], P('chrom'), may hold values from 0.05 to 0.5, as said below
- widths: int32 [8], replicated, may hold values from 1 to 1536, 6144 in all
- ridge_term: float32 [1], replicated, may hold values from 0.5 to 1.5
- direction: float32 [6144, 64], P('samp'), may hold values from -6 to 6
Outputs:
- loco_out: float32 [8, 6144, 64], P('chrom', 'samp')
The draws below stay inside these ranges and needn't reach their ends.
Inputs may be any that keep to these rules, and one draw needn't show every extreme that they name: Each variant's allele frequency is a whole number of thousandths. `genotypes`: each dosage, apart from samples 0 and 1 at variant 0 (set to 2 and 0), is the sum of two independent draws that are 1 with the variant's allele frequency and 0 otherwise. The 8 widths sum to 6144.
All inputs are finite; a program needn't handle non-finite values.
Results may differ from the reference program's by a relative error of at most 0.004.
Values may be sent and summed in bfloat16 or wider, within the bound.
No kernel may reach another device: no remote copies, remote signals or barrier semaphores. Data moves between devices by JAX's collectives and lax.ppermute only.
A program may use at most 64 MiB of HBM per device.

```python
import math
import jax
import jax.numpy as jnp
import numpy as np
from jax import lax

VAR_DEV = 3072
K = 64
SECTIONS = 8
SAMPLES = 6144
VARIANTS = 6144
N_CHROM = 2


def thousandths(key):
    return jax.random.randint(jax.random.fold_in(key, 7301), (VARIANTS,), 50, 501).astype(jnp.int32)


def draw_frequency(key, part):
    return (thousandths(key).astype(jnp.float32) / 1000.0).astype(jnp.float32)


def draw_genotypes(key, part):
    levels = thousandths(key)
    first = jax.random.randint(jax.random.fold_in(key, 7302), (SAMPLES, VARIANTS), 0, 1000)
    second = jax.random.randint(jax.random.fold_in(key, 7303), (SAMPLES, VARIANTS), 0, 1000)
    dosage = (first < levels[None, :]).astype(jnp.int32) + (second < levels[None, :]).astype(jnp.int32)
    dosage = dosage.at[0, 0].set(2)
    dosage = dosage.at[1, 0].set(0)
    return dosage.astype(jnp.int32)


def steps_of(stream_key, shape, pieces, least, top_value):
    def one(dim, shards_of):
        heights = jax.random.uniform(jax.random.fold_in(jax.random.fold_in(stream_key, 6), dim), (shards_of,), jnp.float32, least / len(pieces), top_value / len(pieces))
        return jnp.repeat(jnp.exp(heights), shape[dim] // shards_of).reshape((-1,) + (1,) * (len(shape) - dim - 1))

    loudness = one(*pieces[0])
    for cut in pieces[1:]:
        loudness = loudness * one(*cut)
    return loudness


def length_profile(number_of, total, most, lean):
    portions = [(1 << 20) // math.isqrt(grade ** lean) + 1 for grade in range(2, number_of + 1)]
    rest, counts = total - most - (number_of - 1), [1] * (number_of - 1)
    while rest > 0:
        candidates = [i for i in range(number_of - 1) if counts[i] < most]
        mass, budget = sum([portions[i] for i in candidates]), rest
        for i in candidates:
            addition = min(most - counts[i], max(1, budget * portions[i] // mass), rest)
            counts[i] = counts[i] + addition
            rest = rest - addition
    return np.array([most] + counts)


def ragged(key, count, total, most, lean):
    if count == 2:
        one = jax.random.randint(key, (), max(1, total - most), min(most, total - 1) + 1)
        return jnp.stack([one, total - one])
    lengths = jnp.asarray(length_profile(count, total, most, lean), jnp.int32)
    couples = (count - 1) // 2
    giver, receiver = lengths[1:1 + 2 * couples:2], lengths[2:2 + 2 * couples:2]
    slack = jnp.minimum(giver - 1, most - receiver)
    passed = jax.random.randint(jax.random.fold_in(key, 1), (couples,), 0, 1 << 20) % (slack + 1)
    lengths = lengths.at[1:1 + 2 * couples:2].set(giver - passed).at[2:2 + 2 * couples:2].set(receiver + passed)
    return lengths[jax.random.permutation(jax.random.fold_in(key, 2), count)]


def scatter_about(rng, extent, scale, bound, shards=(), kind=jnp.bfloat16):
    entries = jax.random.normal(rng, extent, jnp.float32) * scale
    if len(shards) > 0:
        entries = steps_of(rng, extent, shards, -0.22, 0.18) * entries
    return jnp.clip(entries, min=-bound, max=bound).astype(kind)


def setup_inputs(seed: int = 0) -> dict:
    seeds = jax.random.split(jax.random.key(seed), 6)
    return {
        "genotypes": draw_genotypes(jax.random.fold_in(seeds[5], 71), 0),
        "frequency": draw_frequency(jax.random.fold_in(seeds[5], 71), 0),
        "widths": ragged(seeds[2], SECTIONS, VARIANTS, VARIANTS // 4, 2).astype(jnp.int32),
        "ridge_term": jnp.clip(jax.random.uniform(seeds[3], (1,), jnp.float32, 0.5, 1.5), 0.5, 1.5),
        "direction": scatter_about(seeds[4], (SAMPLES, K), 1.0, 6.0, ((0, 16),), jnp.float32),
    }


def reference(genotypes, frequency, widths, ridge_term, direction):
    vector = lax.optimization_barrier(direction.astype(jnp.bfloat16)).astype(jnp.float32)
    section_ends = jnp.cumsum(widths).astype(jnp.int32)
    labels = jnp.arange(SECTIONS, dtype=jnp.int32)

    def one_block(running, block_index):
        offset = (block_index * VAR_DEV).astype(jnp.int32)
        dosage = lax.dynamic_slice_in_dim(genotypes, offset, VAR_DEV, 1)
        allele_freq = lax.dynamic_slice_in_dim(frequency, offset, VAR_DEV, 0)
        doubled = 2.0 * allele_freq
        standard = ((dosage.astype(jnp.float32) - doubled) * lax.rsqrt(doubled * (1.0 - allele_freq))).astype(jnp.bfloat16)
        standard = lax.optimization_barrier(standard).astype(jnp.float32)
        crossed = jnp.dot(standard.T, vector, precision=lax.Precision.HIGHEST)
        shared = lax.optimization_barrier(crossed.astype(jnp.bfloat16)).astype(jnp.float32)
        var_index = offset + jnp.arange(VAR_DEV, dtype=jnp.int32)
        section = lax.optimization_barrier(jnp.sum((var_index[:, None] >= section_ends[None, :]).astype(jnp.int32), axis=1))
        onehot = (section[:, None] == labels[None, :]).astype(jnp.float32)
        spread = (shared[:, None, :] * onehot[:, :, None]).reshape(VAR_DEV, SECTIONS * K)
        return (running + jnp.dot(standard, spread, precision=lax.Precision.HIGHEST), None)
    initial = jnp.zeros((SAMPLES, SECTIONS * K), jnp.float32)
    partial_value, _ = lax.scan(one_block, initial, jnp.arange(N_CHROM, dtype=jnp.int32))
    by_section = partial_value.reshape(SAMPLES, SECTIONS, K)
    all_total = lax.optimization_barrier(jnp.sum(by_section, axis=1))
    divisor = (VARIANTS - widths).astype(jnp.float32)
    own_sums = jnp.transpose(by_section, (1, 0, 2))
    return ridge_term[0] * direction[None, :, :] + (all_total[None, :, :] - own_sums) / divisor[:, None, None]
```

```python
import functools

import jax
import jax.numpy as jnp
from jax import lax
from jax.experimental import pallas as pl
from jax.experimental.pallas import tpu as pltpu
from jax.sharding import PartitionSpec as P

VMEM_LIMIT = 24 * 1024 * 1024


def core_and_bits():
    samp = lax.axis_index("samp")
    core = samp % 2
    return core, jnp.where(core == 0, (samp // 2) % 2, (samp // 4) % 2), jnp.where(core == 0, (samp // 4) % 2, (samp // 2) % 2)


def cross_kernel(blocks, geno_hbm, freq_ref, dir_ref, stand_ref, keep_ref, send_ref, geno, sems):
    width = geno_hbm.shape[1] // blocks
    copies = []
    for i in range(blocks):
        columns = pl.ds(i * width, width)
        copies.append(pltpu.make_async_copy(geno_hbm.at[:, columns], geno.at[:, columns], sems.at[i]))
        copies[-1].start()
    half = dir_ref.shape[0] // 2
    first = lax.axis_index("samp") % 2 == 0
    vector = dir_ref[...].astype(jnp.bfloat16)
    for i in range(blocks):
        columns = pl.ds(i * width, width)
        doubled = 2.0 * freq_ref[:, columns]
        scale = lax.rsqrt(doubled * (1.0 - freq_ref[:, columns]))
        copies[i].wait()
        standard = ((geno[:, columns].astype(jnp.float32) - doubled) * scale).astype(jnp.bfloat16)
        stand_ref[:, columns] = standard
        crossed = jnp.dot(vector, standard, preferred_element_type=jnp.float32)
        keep_ref[:, columns] = jnp.where(first, crossed[:half], crossed[half:])
        send_ref[:, columns] = jnp.where(first, crossed[half:], crossed[:half]).astype(jnp.bfloat16)


def section_kernel(others, widths_ref, stand_ref, *refs):
    *pieces, out_ref = refs
    variants = stand_ref.shape[1]
    sections = widths_ref.shape[0]
    chrom = lax.axis_index("chrom")
    half = (chrom // (lax.axis_size("chrom") // 2)) % 2
    first_section = (1 - half if others else half) * (sections // 2)
    first_var = chrom * variants
    var = first_var + lax.broadcasted_iota(jnp.int32, (1, variants), 1)
    start = jnp.int32(0)
    for c in range(sections // 2):
        start = start + jnp.where(first_section > 0, widths_ref[c], 0)
    shared = jnp.concatenate([p[...] for p in pieces], axis=0)
    spread = []
    for c in range(sections // 2):
        end = start + widths_ref[first_section + c]
        outside = jnp.where((var < start) | (var >= end), 1.0, 0.0).astype(jnp.bfloat16)
        spread.append(shared * outside)
        start = end
    product = lax.dot_general(
        jnp.concatenate(spread, axis=0), stand_ref[...], (((1,), (1,)), ((), ())), preferred_element_type=jnp.float32
    )
    out_ref[...] = product.reshape(out_ref.shape).astype(out_ref.dtype)


def finish_kernel(total, widths_ref, ridge_ref, dir_ref, own_ref, got_ref, out_ref):
    per_device, rhs, _ = out_ref.shape
    first_section = lax.axis_index("chrom") * per_device
    core, mine, sibling = core_and_bits()
    quarter = rhs // 4
    half = rhs // 2
    rows = [
        core * half + mine * quarter,
        core * half + (1 - mine) * quarter,
        (1 - core) * half + sibling * quarter,
        (1 - core) * half + (1 - sibling) * quarter,
    ]
    for p in range(4):
        at = pl.ds(pl.multiple_of(rows[p], quarter), quarter)
        ridged = ridge_ref[0] * dir_ref[at, :]
        here = pl.ds(p * quarter, quarter)
        for c in range(per_device):
            divisor = (total - widths_ref[first_section + c]).astype(jnp.float32)
            rest = own_ref[c, here, :] + got_ref[c, here, :].astype(jnp.float32)
            out_ref[c, at, :] = ridged + rest / divisor


def on_device(genotypes, frequency, widths, ridge_term, direction):
    rows, variants = genotypes.shape
    rhs = direction.shape[1]
    sections = widths.shape[0]
    n_samp, n_chrom = lax.axis_size("samp"), lax.axis_size("chrom")
    per_device = sections // n_chrom
    half, quarter = rhs // 2, rhs // 4
    vmem = pl.BlockSpec(memory_space=pltpu.VMEM)
    smem = pl.BlockSpec(memory_space=pltpu.SMEM)
    params = pltpu.CompilerParams(vmem_limit_bytes=VMEM_LIMIT)
    dir_t = direction.T

    blocks = max(1, variants // 512)
    standard, keep, send = pl.pallas_call(
        functools.partial(cross_kernel, blocks),
        out_shape=(
            jax.ShapeDtypeStruct((rows, variants), jnp.bfloat16),
            jax.ShapeDtypeStruct((half, variants), jnp.float32),
            jax.ShapeDtypeStruct((half, variants), jnp.bfloat16),
        ),
        in_specs=[pl.BlockSpec(memory_space=pl.ANY), vmem, vmem],
        out_specs=(vmem, vmem, vmem),
        scratch_shapes=[pltpu.VMEM((rows, variants), jnp.int32), pltpu.SemaphoreType.DMA((blocks,))],
        compiler_params=params,
        name="cross",
    )(genotypes, frequency.reshape(1, variants), dir_t)

    def swap(x, even, odd):
        return lax.ppermute(x, "samp", [(i, i ^ (odd if i % 2 else even)) for i in range(n_samp)])

    core, mine, _ = core_and_bits()
    sums = keep + swap(send, 1, 1)
    at = lambda b: lax.dynamic_slice_in_dim(sums, b * quarter, quarter, 0)
    mine_sum = at(mine) + swap(at(1 - mine).astype(jnp.bfloat16), 2, 4)
    mine_sum = mine_sum + swap(mine_sum.astype(jnp.bfloat16), 4, 2)
    bit = 8
    while bit < n_samp:
        mine_sum = mine_sum + swap(mine_sum.astype(jnp.bfloat16), bit, bit)
        bit *= 2
    first = mine_sum.astype(jnp.bfloat16)
    second = swap(first, 2, 4)
    pieces = (first, second, swap(first, 1, 1), swap(second, 1, 1))

    def products(others, dtype):
        return pl.pallas_call(
            functools.partial(section_kernel, others),
            out_shape=jax.ShapeDtypeStruct((sections // 2, rhs, rows), dtype),
            in_specs=[smem, vmem] + [vmem] * 4,
            out_specs=vmem,
            compiler_params=params,
            cost_estimate=pl.CostEstimate(
                flops=rows * variants * rhs * sections, bytes_accessed=rows * variants * 2, transcendentals=0
            ),
            name="others" if others else "own",
        )(widths, standard, *pieces)

    def swap_chrom(x, bit):
        return lax.ppermute(x, "chrom", [(i, i ^ bit) for i in range(n_chrom)])

    bit = n_chrom // 2
    got = swap_chrom(products(True, jnp.bfloat16), bit)
    own = products(False, jnp.float32)
    while bit > 1:
        own = own + got
        bit //= 2
        count = own.shape[0] // 2
        side = (lax.axis_index("chrom") // bit) % 2
        got = swap_chrom(lax.dynamic_slice_in_dim(own, (1 - side) * count, count, 0).astype(jnp.bfloat16), bit)
        own = lax.dynamic_slice_in_dim(own, side * count, count, 0)

    out = pl.pallas_call(
        functools.partial(finish_kernel, variants * n_chrom),
        out_shape=jax.ShapeDtypeStruct((per_device, rhs, rows), jnp.float32),
        in_specs=[smem, smem, vmem, vmem, vmem],
        out_specs=vmem,
        compiler_params=params,
        name="finish",
    )(widths, ridge_term, dir_t, own, got)
    return jnp.transpose(out, (0, 2, 1))


def solution(mesh):
    return jax.shard_map(
        on_device,
        mesh=mesh,
        in_specs=(P("samp", "chrom"), P("chrom"), P(), P(), P("samp", None)),
        out_specs=P("chrom", "samp", None),
        check_vma=False,
    )
```

```python
import functools

import jax
import jax.numpy as jnp
from jax import lax
from jax.experimental import pallas as pl
from jax.experimental.pallas import tpu as pltpu
from jax.sharding import PartitionSpec as P

VMEM_LIMIT = 24 * 1024 * 1024
BLOCK = 512


def core_and_bits():
    samp = lax.axis_index("samp")
    core, y, z = samp % 2, (samp // 2) % 2, (samp // 4) % 2
    return core, jnp.where(core == 0, y, z), jnp.where(core == 0, z, y)


def cross_kernel(blocks, geno_hbm, freq_hbm, dir_hbm, stand_ref, keep_ref, send_ref, geno, freq_ref, dir_ref, sems):
    width = geno_hbm.shape[1] // blocks
    small = [
        pltpu.make_async_copy(freq_hbm, freq_ref, sems.at[blocks]),
        pltpu.make_async_copy(dir_hbm, dir_ref, sems.at[blocks + 1]),
    ]
    for copy in small:
        copy.start()
    copies = []
    for i in range(blocks):
        columns = pl.ds(i * width, width)
        copies.append(pltpu.make_async_copy(geno_hbm.at[:, columns], geno.at[:, columns], sems.at[i]))
        copies[-1].start()
    half = dir_ref.shape[0] // 2
    first = lax.axis_index("samp") % 2 == 0
    for copy in small:
        copy.wait()
    vector = dir_ref[...].astype(jnp.bfloat16)
    for i in range(blocks):
        columns = pl.ds(i * width, width)
        doubled = 2.0 * freq_ref[:, columns]
        scale = lax.rsqrt(doubled * (1.0 - freq_ref[:, columns]))
        copies[i].wait()
        standard = ((geno[:, columns].astype(jnp.float32) - doubled) * scale).astype(jnp.bfloat16)
        stand_ref[:, columns] = standard
        crossed = jnp.dot(vector, standard, preferred_element_type=jnp.float32)
        keep_ref[:, columns] = jnp.where(first, crossed[:half], crossed[half:])
        send_ref[:, columns] = jnp.where(first, crossed[half:], crossed[:half]).astype(jnp.bfloat16)


def piece_rows(rhs):
    core, mine, sibling = core_and_bits()
    half, quarter = rhs // 2, rhs // 4
    return [
        core * half + mine * quarter,
        (1 - core) * half + sibling * quarter,
        core * half + (1 - mine) * quarter,
        (1 - core) * half + (1 - sibling) * quarter,
    ]


def prepare_kernel(total, widths_ref, ridge_ref, dir_ref, others_ref, own_ref, inverse_ref, ridged_ref):
    sections = widths_ref.shape[0]
    _, rows, variants = own_ref.shape
    per_device = inverse_ref.shape[0]
    rhs = dir_ref.shape[0]
    chrom = lax.axis_index("chrom")
    side = (chrom // (lax.axis_size("chrom") // 2)) % 2
    var = chrom * variants + lax.broadcasted_iota(jnp.int32, (1, variants), 1)
    start = jnp.int32(0)
    for c in range(sections):
        end = start + widths_ref[c]
        outside = jnp.where((var < start) | (var >= end), 1.0, 0.0)
        outside = jnp.broadcast_to(outside, (rows, variants)).astype(jnp.bfloat16)
        here = side == (0 if c < sections // 2 else 1)

        @pl.when(here)
        def _():
            own_ref[c % (sections // 2)] = outside

        @pl.when(jnp.logical_not(here))
        def _():
            others_ref[c % (sections // 2)] = outside

        start = end
    for c in range(per_device):
        divisor = (total - widths_ref[chrom * per_device + c]).astype(jnp.float32)
        inverse_ref[c] = 1.0 / jnp.full(inverse_ref.shape[1:], divisor, jnp.float32)
    for p, row in enumerate(piece_rows(rhs)):
        quarter = rhs // 4
        ridged_ref[pl.ds(p * quarter, quarter), :] = ridge_ref[0] * dir_ref[pl.ds(pl.multiple_of(row, quarter), quarter), :]


def section_kernel(outside_ref, stand_ref, *refs):
    *pieces, out_ref = refs
    count = outside_ref.shape[0]
    spread = [p[...] * outside_ref[c] for c in range(count) for p in pieces]
    product = lax.dot_general(
        jnp.concatenate(spread, axis=0), stand_ref[...], (((1,), (1,)), ((), ())), preferred_element_type=jnp.float32
    )
    out_ref[...] = product.reshape(out_ref.shape).astype(out_ref.dtype)


def finish_kernel(inverse_ref, ridged_ref, *refs):
    owns, gots, out_ref = refs[:2], refs[2:4], refs[4]
    per_device, rhs, _ = out_ref.shape
    quarter = rhs // 4
    for p, row in enumerate(piece_rows(rhs)):
        at = pl.ds(pl.multiple_of(row, quarter), quarter)
        ridged = ridged_ref[pl.ds(p * quarter, quarter), :]
        here = pl.ds((p % 2) * quarter, quarter)
        for c in range(per_device):
            rest = owns[p // 2][c, here, :] + gots[p // 2][c, here, :].astype(jnp.float32)
            out_ref[c, at, :] = ridged + rest * inverse_ref[c]


def on_device(genotypes, frequency, widths, ridge_term, direction):
    rows, variants = genotypes.shape
    rhs = direction.shape[1]
    sections = widths.shape[0]
    n_samp, n_chrom = lax.axis_size("samp"), lax.axis_size("chrom")
    per_device = sections // n_chrom
    half, quarter = rhs // 2, rhs // 4
    vmem = pl.BlockSpec(memory_space=pltpu.VMEM)
    smem = pl.BlockSpec(memory_space=pltpu.SMEM)
    params = pltpu.CompilerParams(vmem_limit_bytes=VMEM_LIMIT)
    dir_t = direction.T

    blocks = max(1, variants // BLOCK)
    operands = (genotypes, frequency.reshape(1, variants), dir_t)
    standard, keep, send = pl.pallas_call(
        functools.partial(cross_kernel, blocks),
        out_shape=(
            jax.ShapeDtypeStruct((rows, variants), jnp.bfloat16),
            jax.ShapeDtypeStruct((half, variants), jnp.float32),
            jax.ShapeDtypeStruct((half, variants), jnp.bfloat16),
        ),
        in_specs=[pl.BlockSpec(memory_space=pl.ANY)] * 3,
        out_specs=(vmem, vmem, vmem),
        scratch_shapes=[
            pltpu.VMEM((rows, variants), jnp.int32),
            pltpu.VMEM((1, variants), jnp.float32),
            pltpu.VMEM((rhs, rows), jnp.float32),
            pltpu.SemaphoreType.DMA((blocks + 2,)),
        ],
        compiler_params=params,
        name="cross",
    )(*(pltpu.with_memory_space_constraint(a, pltpu.HBM) for a in operands))

    mask = jax.ShapeDtypeStruct((sections // 2, quarter, variants), jnp.bfloat16)
    outside_others, outside_own, inverse, ridged = pl.pallas_call(
        functools.partial(prepare_kernel, variants * n_chrom),
        out_shape=(
            mask,
            mask,
            jax.ShapeDtypeStruct((per_device, quarter, rows), jnp.float32),
            jax.ShapeDtypeStruct((rhs, rows), jnp.float32),
        ),
        in_specs=[smem, smem, vmem],
        out_specs=(vmem,) * 4,
        compiler_params=params,
        name="prepare",
    )(widths, ridge_term, dir_t)

    def swap(x, even, odd):
        return lax.ppermute(x, "samp", [(i, i ^ (odd if i % 2 else even)) for i in range(n_samp)])

    _, mine, _ = core_and_bits()
    sums = keep + swap(send, 1, 1)
    at = lambda b: lax.dynamic_slice_in_dim(sums, b * quarter, quarter, 0)
    mine_sum = at(mine) + swap(at(1 - mine).astype(jnp.bfloat16), 2, 4)
    mine_sum, outside_others, outside_own, inverse, ridged = lax.optimization_barrier(
        (mine_sum, outside_others, outside_own, inverse, ridged)
    )
    rest = [1 << b for b in range(3, n_samp.bit_length() - 1)]
    even_bits, odd_bits = [4] + rest, [2] + rest
    for even, odd in zip(even_bits, odd_bits):
        mine_sum = mine_sum + swap(mine_sum.astype(jnp.bfloat16), even, odd)
    first = mine_sum.astype(jnp.bfloat16)
    second = swap(first, 2, 4)
    halves = ((first, swap(first, 1, 1)), (second, swap(second, 1, 1)))

    def products(outside, pieces, dtype, name):
        return pl.pallas_call(
            section_kernel,
            out_shape=jax.ShapeDtypeStruct((sections // 2, half, rows), dtype),
            in_specs=[vmem] * 4,
            out_specs=vmem,
            compiler_params=params,
            cost_estimate=pl.CostEstimate(
                flops=rows * variants * half * sections, bytes_accessed=rows * variants * 2, transcendentals=0
            ),
            name=name,
        )(outside, standard, *pieces)

    def swap_chrom(x, bit):
        return lax.ppermute(x, "chrom", [(i, i ^ bit) for i in range(n_chrom)])

    bit = n_chrom // 2
    gots = [swap_chrom(products(outside_others, pieces, jnp.bfloat16, "others"), bit) for pieces in halves]
    owns = [products(outside_own, pieces, jnp.float32, "own") for pieces in halves]
    while bit > 1:
        bit //= 2
        count = owns[0].shape[0] // 2
        side = (lax.axis_index("chrom") // bit) % 2
        sums = [own + got for own, got in zip(owns, gots)]
        gots = [
            swap_chrom(lax.dynamic_slice_in_dim(s, (1 - side) * count, count, 0).astype(jnp.bfloat16), bit) for s in sums
        ]
        owns = [lax.dynamic_slice_in_dim(s, side * count, count, 0) for s in sums]

    out = pl.pallas_call(
        finish_kernel,
        out_shape=jax.ShapeDtypeStruct((per_device, rhs, rows), jnp.float32),
        in_specs=[vmem] * 6,
        out_specs=vmem,
        compiler_params=params,
        name="finish",
    )(inverse, ridged, *owns, *gots)
    return jnp.transpose(out, (0, 2, 1))


def solution(mesh):
    return jax.shard_map(
        on_device,
        mesh=mesh,
        in_specs=(P("samp", "chrom"), P("chrom"), P(), P(), P("samp", None)),
        out_specs=P("chrom", "samp", None),
        check_vma=False,
    )
```

```python
import functools

import jax
import jax.numpy as jnp
from jax import lax
from jax.experimental import pallas as pl
from jax.experimental.pallas import tpu as pltpu
from jax.sharding import PartitionSpec as P

VMEM_LIMIT = 24 * 1024 * 1024
BLOCK = 512


def core_and_bits():
    samp = lax.axis_index("samp")
    core, y, z = samp % 2, (samp // 2) % 2, (samp // 4) % 2
    return core, jnp.where(core == 0, y, z), jnp.where(core == 0, z, y)


def cross_kernel(blocks, geno_hbm, freq_hbm, dir_hbm, stand_ref, keep_ref, send_ref, geno, freq_ref, dir_ref, sems):
    width = geno_hbm.shape[1] // blocks
    small = [
        pltpu.make_async_copy(freq_hbm, freq_ref, sems.at[blocks]),
        pltpu.make_async_copy(dir_hbm, dir_ref, sems.at[blocks + 1]),
    ]
    for copy in small:
        copy.start()
    copies = []
    for i in range(blocks):
        columns = pl.ds(i * width, width)
        copies.append(pltpu.make_async_copy(geno_hbm.at[:, columns], geno.at[:, columns], sems.at[i]))
        copies[-1].start()
    half = dir_ref.shape[0] // 2
    first = lax.axis_index("samp") % 2 == 0
    for copy in small:
        copy.wait()
    vector = dir_ref[...].astype(jnp.bfloat16)
    for i in range(blocks):
        columns = pl.ds(i * width, width)
        doubled = 2.0 * freq_ref[:, columns]
        scale = lax.rsqrt(doubled * (1.0 - freq_ref[:, columns]))
        copies[i].wait()
        standard = ((geno[:, columns].astype(jnp.float32) - doubled) * scale).astype(jnp.bfloat16)
        stand_ref[:, columns] = standard
        crossed = jnp.dot(vector, standard, preferred_element_type=jnp.float32)
        keep_ref[:, columns] = jnp.where(first, crossed[:half], crossed[half:])
        send_ref[:, columns] = jnp.where(first, crossed[half:], crossed[:half]).astype(jnp.bfloat16)


def piece_rows(rhs):
    core, mine, sibling = core_and_bits()
    half, quarter = rhs // 2, rhs // 4
    return [
        core * half + mine * quarter,
        (1 - core) * half + sibling * quarter,
        core * half + (1 - mine) * quarter,
        (1 - core) * half + (1 - sibling) * quarter,
    ]


def prepare_kernel(total, widths_ref, ridge_ref, dir_ref, others_ref, own_ref, inverse_ref, ridged_ref):
    sections = widths_ref.shape[0]
    _, rows, variants = own_ref.shape
    per_device = inverse_ref.shape[0]
    near = others_ref.shape[0]
    rhs = dir_ref.shape[0]
    chrom = lax.axis_index("chrom")
    side = (chrom // (lax.axis_size("chrom") // 2)) % 2
    var = chrom * variants + lax.broadcasted_iota(jnp.int32, (1, variants), 1)
    start = jnp.int32(0)
    for c in range(sections):
        end = start + widths_ref[c]
        outside = jnp.where((var < start) | (var >= end), 1.0, 0.0)
        outside = jnp.broadcast_to(outside, (rows, variants)).astype(jnp.bfloat16)
        here = side == (0 if c < sections // 2 else 1)

        @pl.when(here)
        def _():
            own_ref[c % (sections // 2)] = outside

        if sections // 2 - near <= c < sections // 2 + near:

            @pl.when(jnp.logical_not(here))
            def _():
                others_ref[c - (sections // 2 - near if c < sections // 2 else sections // 2)] = outside

        start = end
    for c in range(per_device):
        divisor = (total - widths_ref[chrom * per_device + c]).astype(jnp.float32)
        inverse_ref[c] = 1.0 / jnp.full(inverse_ref.shape[1:], divisor, jnp.float32)
    for p, row in enumerate(piece_rows(rhs)):
        quarter = rhs // 4
        ridged_ref[pl.ds(p * quarter, quarter), :] = ridge_ref[0] * dir_ref[pl.ds(pl.multiple_of(row, quarter), quarter), :]


def section_kernel(outside_ref, stand_ref, *refs):
    *pieces, out_ref = refs
    count = outside_ref.shape[0]
    spread = [p[...] for p in pieces] if out_ref.shape[0] > count else []
    spread += [p[...] * outside_ref[c] for c in range(count) for p in pieces]
    product = lax.dot_general(
        jnp.concatenate(spread, axis=0), stand_ref[...], (((1,), (1,)), ((), ())), preferred_element_type=jnp.float32
    )
    out_ref[...] = product.reshape(out_ref.shape).astype(out_ref.dtype)


def received(c, sections, near, side):
    if sections // 2 <= near:
        return c + 1
    low = c - (sections // 2 - near) + 1
    return jnp.where(side == 0, max(low, 0), c + 1 if c < near else 0)


def finish_kernel(near, inverse_ref, ridged_ref, *refs):
    owns, gots, out_ref = refs[:2], refs[2:4], refs[4]
    per_device, rhs, _ = out_ref.shape
    side = lax.axis_index("chrom")
    places = [received(c, 2 * per_device, near, side) if near else c for c in range(per_device)]
    quarter = rhs // 4
    for p, row in enumerate(piece_rows(rhs)):
        at = pl.ds(pl.multiple_of(row, quarter), quarter)
        ridged = ridged_ref[pl.ds(p * quarter, quarter), :]
        here = pl.ds((p % 2) * quarter, quarter)
        for c in range(per_device):
            rest = owns[p // 2][c, here, :] + gots[p // 2][places[c], here, :].astype(jnp.float32)
            out_ref[c, at, :] = ridged + rest * inverse_ref[c]


def on_device(genotypes, frequency, widths, ridge_term, direction):
    rows, variants = genotypes.shape
    rhs = direction.shape[1]
    sections = widths.shape[0]
    n_samp, n_chrom = lax.axis_size("samp"), lax.axis_size("chrom")
    per_device = sections // n_chrom
    half, quarter = rhs // 2, rhs // 4
    vmem = pl.BlockSpec(memory_space=pltpu.VMEM)
    smem = pl.BlockSpec(memory_space=pltpu.SMEM)
    params = pltpu.CompilerParams(vmem_limit_bytes=VMEM_LIMIT)
    dir_t = direction.T

    blocks = max(1, variants // BLOCK)
    operands = (genotypes, frequency.reshape(1, variants), dir_t)
    standard, keep, send = pl.pallas_call(
        functools.partial(cross_kernel, blocks),
        out_shape=(
            jax.ShapeDtypeStruct((rows, variants), jnp.bfloat16),
            jax.ShapeDtypeStruct((half, variants), jnp.float32),
            jax.ShapeDtypeStruct((half, variants), jnp.bfloat16),
        ),
        in_specs=[pl.BlockSpec(memory_space=pl.ANY)] * 3,
        out_specs=(vmem, vmem, vmem),
        scratch_shapes=[
            pltpu.VMEM((rows, variants), jnp.int32),
            pltpu.VMEM((1, variants), jnp.float32),
            pltpu.VMEM((rhs, rows), jnp.float32),
            pltpu.SemaphoreType.DMA((blocks + 2,)),
        ],
        compiler_params=params,
        name="cross",
    )(*(pltpu.with_memory_space_constraint(a, pltpu.HBM) for a in operands))

    near = max(1, sections // 4)
    mask = lambda count: jax.ShapeDtypeStruct((count, quarter, variants), jnp.bfloat16)
    outside_others, outside_own, inverse, ridged = pl.pallas_call(
        functools.partial(prepare_kernel, variants * n_chrom),
        out_shape=(
            mask(near),
            mask(sections // 2),
            jax.ShapeDtypeStruct((per_device, quarter, rows), jnp.float32),
            jax.ShapeDtypeStruct((rhs, rows), jnp.float32),
        ),
        in_specs=[smem, smem, vmem],
        out_specs=(vmem,) * 4,
        compiler_params=params,
        name="prepare",
    )(widths, ridge_term, dir_t)

    def swap(x, even, odd):
        return lax.ppermute(x, "samp", [(i, i ^ (odd if i % 2 else even)) for i in range(n_samp)])

    _, mine, _ = core_and_bits()
    sums = keep + swap(send, 1, 1)
    at = lambda b: lax.dynamic_slice_in_dim(sums, b * quarter, quarter, 0)
    mine_sum = at(mine) + swap(at(1 - mine).astype(jnp.bfloat16), 2, 4)
    mine_sum, outside_others, outside_own, inverse, ridged = lax.optimization_barrier(
        (mine_sum, outside_others, outside_own, inverse, ridged)
    )
    rest = [1 << b for b in range(3, n_samp.bit_length() - 1)]
    even_bits, odd_bits = [4] + rest, [2] + rest
    for even, odd in zip(even_bits, odd_bits):
        mine_sum = mine_sum + swap(mine_sum.astype(jnp.bfloat16), even, odd)
    first = mine_sum.astype(jnp.bfloat16)
    second = swap(first, 2, 4)

    def products(outside, pieces, count, dtype, name):
        return pl.pallas_call(
            section_kernel,
            out_shape=jax.ShapeDtypeStruct((count, half, rows), dtype),
            in_specs=[vmem] * 4,
            out_specs=vmem,
            compiler_params=params,
            cost_estimate=pl.CostEstimate(
                flops=rows * variants * half * sections, bytes_accessed=rows * variants * 2, transcendentals=0
            ),
            name=name,
        )(outside, standard, *pieces)

    def swap_chrom(x, bit):
        return lax.ppermute(x, "chrom", [(i, i ^ bit) for i in range(n_chrom)])

    bit = n_chrom // 2
    for_others = lambda pieces: products(outside_others, pieces, near + 1, jnp.bfloat16, "others")
    head = (first, swap(first, 1, 1))
    products_head = for_others(head)
    second, products_head = lax.optimization_barrier((second, products_head))
    tail = (second, swap(second, 1, 1))
    gots = [swap_chrom(products_head, bit), swap_chrom(for_others(tail), bit)]
    owns = [products(outside_own, pieces, sections // 2, jnp.float32, "own") for pieces in (head, tail)]
    if bit > 1:
        side = (lax.axis_index("chrom") // bit) % 2
        places = [received(c, sections, near, side) for c in range(sections // 2)]
        gots = [jnp.stack([lax.dynamic_index_in_dim(got, p, 0, False) for p in places]) for got in gots]
    while bit > 1:
        bit //= 2
        count = owns[0].shape[0] // 2
        side = (lax.axis_index("chrom") // bit) % 2
        sums = [own + got for own, got in zip(owns, gots)]
        gots = [
            swap_chrom(lax.dynamic_slice_in_dim(s, (1 - side) * count, count, 0).astype(jnp.bfloat16), bit) for s in sums
        ]
        owns = [lax.dynamic_slice_in_dim(s, side * count, count, 0) for s in sums]

    out = pl.pallas_call(
        functools.partial(finish_kernel, near if n_chrom == 2 else 0),
        out_shape=jax.ShapeDtypeStruct((per_device, rhs, rows), jnp.float32),
        in_specs=[vmem] * 6,
        out_specs=vmem,
        compiler_params=params,
        name="finish",
    )(inverse, ridged, *owns, *gots)
    return jnp.transpose(out, (0, 2, 1))


def solution(mesh):
    return jax.shard_map(
        on_device,
        mesh=mesh,
        in_specs=(P("samp", "chrom"), P("chrom"), P(), P(), P("samp", None)),
        out_specs=P("chrom", "samp", None),
        check_vma=False,
    )
```

```python
import functools

import jax
import jax.numpy as jnp
from jax import lax
from jax.experimental import pallas as pl
from jax.experimental.pallas import tpu as pltpu
from jax.sharding import PartitionSpec as P

VMEM_LIMIT = 24 * 1024 * 1024
BLOCK = 512


def core_and_bits():
    samp = lax.axis_index("samp")
    core, y, z = samp % 2, (samp // 2) % 2, (samp // 4) % 2
    return core, jnp.where(core == 0, y, z), jnp.where(core == 0, z, y)


def piece_rows(rhs):
    core, mine, sibling = core_and_bits()
    half, quarter = rhs // 2, rhs // 4
    return [
        core * half + mine * quarter,
        (1 - core) * half + sibling * quarter,
        core * half + (1 - mine) * quarter,
        (1 - core) * half + (1 - sibling) * quarter,
    ]


def cross_kernel(blocks, geno_hbm, freq_hbm, dir_hbm, stand_ref, *refs):
    quarters, (geno, freq_ref, dir_ref, sems) = refs[:4], refs[4:]
    width = geno_hbm.shape[1] // blocks
    small = [
        pltpu.make_async_copy(freq_hbm, freq_ref, sems.at[blocks]),
        pltpu.make_async_copy(dir_hbm, dir_ref, sems.at[blocks + 1]),
    ]
    for copy in small:
        copy.start()
    copies = []
    for i in range(blocks):
        columns = pl.ds(i * width, width)
        copies.append(pltpu.make_async_copy(geno_hbm.at[:, columns], geno.at[:, columns], sems.at[i]))
        copies[-1].start()
    quarter = dir_ref.shape[0] // 4
    mine, sibling, sent, sibling_sent = piece_rows(dir_ref.shape[0])
    for copy in small:
        copy.wait()
    vector = jnp.concatenate(
        [dir_ref[pl.ds(pl.multiple_of(row, quarter), quarter), :] for row in (sibling_sent, sibling, sent, mine)], axis=0
    ).astype(jnp.bfloat16)
    for i in range(blocks):
        columns = pl.ds(i * width, width)
        doubled = 2.0 * freq_ref[:, columns]
        scale = lax.rsqrt(doubled * (1.0 - freq_ref[:, columns]))
        copies[i].wait()
        standard = ((geno[:, columns].astype(jnp.float32) - doubled) * scale).astype(jnp.bfloat16)
        stand_ref[:, columns] = standard
        crossed = jnp.dot(vector, standard, preferred_element_type=jnp.float32)
        for q, ref in enumerate(quarters):
            ref[:, columns] = crossed[q * quarter : (q + 1) * quarter].astype(ref.dtype)


def prepare_kernel(total, widths_ref, ridge_ref, dir_ref, others_ref, own_ref, inverse_ref, ridged_ref):
    sections = widths_ref.shape[0]
    _, rows, variants = own_ref.shape
    per_device = inverse_ref.shape[0]
    near = others_ref.shape[0]
    rhs = dir_ref.shape[0]
    chrom = lax.axis_index("chrom")
    side = (chrom // (lax.axis_size("chrom") // 2)) % 2
    var = chrom * variants + lax.broadcasted_iota(jnp.int32, (1, variants), 1)
    start = jnp.int32(0)
    for c in range(sections):
        end = start + widths_ref[c]
        outside = jnp.where((var < start) | (var >= end), 1.0, 0.0)
        outside = jnp.broadcast_to(outside, (rows, variants)).astype(jnp.bfloat16)
        here = side == (0 if c < sections // 2 else 1)

        @pl.when(here)
        def _():
            own_ref[c % (sections // 2)] = outside

        if sections // 2 - near <= c < sections // 2 + near:

            @pl.when(jnp.logical_not(here))
            def _():
                others_ref[c - (sections // 2 - near if c < sections // 2 else sections // 2)] = outside

        start = end
    for c in range(per_device):
        divisor = (total - widths_ref[chrom * per_device + c]).astype(jnp.float32)
        inverse_ref[c] = 1.0 / jnp.full(inverse_ref.shape[1:], divisor, jnp.float32)
    for p, row in enumerate(piece_rows(rhs)):
        quarter = rhs // 4
        ridged_ref[pl.ds(p * quarter, quarter), :] = ridge_ref[0] * dir_ref[pl.ds(pl.multiple_of(row, quarter), quarter), :]


def received(c, sections, near, side):
    if sections // 2 <= near:
        return c + 1
    low = c - (sections // 2 - near) + 1
    return jnp.where(side == 0, max(low, 0), c + 1 if c < near else 0)


def section_kernel(near, outside_ref, stand_ref, *refs):
    pieces, got_ref, out_ref = refs[:2], refs[2], refs[-1]
    count = outside_ref.shape[0]
    spread = [p[...] for p in pieces] if out_ref.shape[0] > count else []
    spread += [p[...] * outside_ref[c] for c in range(count) for p in pieces]
    product = lax.dot_general(
        jnp.concatenate(spread, axis=0), stand_ref[...], (((1,), (1,)), ((), ())), preferred_element_type=jnp.float32
    )
    product = product.reshape(out_ref.shape)
    if not near:
        out_ref[...] = product.astype(out_ref.dtype)
        return
    side = lax.axis_index("chrom")
    for c in range(count):
        out_ref[c] = product[c] + got_ref[received(c, 2 * count, near, side)].astype(jnp.float32)


def finish_kernel(near, inverse_ref, ridged_ref, *refs):
    head_ref, tail_ref, got_ref, out_ref = refs
    per_device, rhs, _ = out_ref.shape
    side = lax.axis_index("chrom")
    places = [received(c, 2 * per_device, near, side) if near else c for c in range(per_device)]
    quarter = rhs // 4
    for p, row in enumerate(piece_rows(rhs)):
        at = pl.ds(pl.multiple_of(row, quarter), quarter)
        ridged = ridged_ref[pl.ds(p * quarter, quarter), :]
        here = pl.ds((p % 2) * quarter, quarter)
        for c in range(per_device):
            if p < 2:
                rest = head_ref[c, here, :]
            else:
                rest = tail_ref[c, here, :] + got_ref[places[c], here, :].astype(jnp.float32)
            out_ref[c, at, :] = ridged + rest * inverse_ref[c]


def on_device(genotypes, frequency, widths, ridge_term, direction):
    rows, variants = genotypes.shape
    rhs = direction.shape[1]
    sections = widths.shape[0]
    n_samp, n_chrom = lax.axis_size("samp"), lax.axis_size("chrom")
    per_device = sections // n_chrom
    half, quarter = rhs // 2, rhs // 4
    vmem = pl.BlockSpec(memory_space=pltpu.VMEM)
    smem = pl.BlockSpec(memory_space=pltpu.SMEM)
    params = pltpu.CompilerParams(vmem_limit_bytes=VMEM_LIMIT)
    dir_t = direction.T

    blocks = max(1, variants // BLOCK)
    operands = (genotypes, frequency.reshape(1, variants), dir_t)
    parts = [jax.ShapeDtypeStruct((quarter, variants), dtype) for dtype in (jnp.bfloat16, jnp.float32)]
    standard, give_first, give_second, keep_first, keep_second = pl.pallas_call(
        functools.partial(cross_kernel, blocks),
        out_shape=(
            jax.ShapeDtypeStruct((rows, variants), jnp.bfloat16),
            *(parts[i] for i in (0, 0, 1, 1)),
        ),
        in_specs=[pl.BlockSpec(memory_space=pl.ANY)] * 3,
        out_specs=(vmem,) * 5,
        scratch_shapes=[
            pltpu.VMEM((rows, variants), jnp.int32),
            pltpu.VMEM((1, variants), jnp.float32),
            pltpu.VMEM((rhs, rows), jnp.float32),
            pltpu.SemaphoreType.DMA((blocks + 2,)),
        ],
        compiler_params=params,
        name="cross",
    )(*(pltpu.with_memory_space_constraint(a, pltpu.HBM) for a in operands))

    near = max(1, sections // 4)
    mask = lambda count: jax.ShapeDtypeStruct((count, quarter, variants), jnp.bfloat16)
    outside_others, outside_own, inverse, ridged = pl.pallas_call(
        functools.partial(prepare_kernel, variants * n_chrom),
        out_shape=(
            mask(near),
            mask(sections // 2),
            jax.ShapeDtypeStruct((per_device, quarter, rows), jnp.float32),
            jax.ShapeDtypeStruct((rhs, rows), jnp.float32),
        ),
        in_specs=[smem, smem, vmem],
        out_specs=(vmem,) * 4,
        compiler_params=params,
        name="prepare",
    )(widths, ridge_term, dir_t)

    def swap(x, even, odd):
        return lax.ppermute(x, "samp", [(i, i ^ (odd if i % 2 else even)) for i in range(n_samp)])

    sent = (keep_first + swap(give_first, 1, 1)).astype(jnp.bfloat16)
    mine_sum = keep_second + swap(give_second, 1, 1) + swap(sent, 2, 4)
    mine_sum, outside_others, outside_own, inverse, ridged = lax.optimization_barrier(
        (mine_sum, outside_others, outside_own, inverse, ridged)
    )
    rest = [1 << b for b in range(3, n_samp.bit_length() - 1)]
    even_bits, odd_bits = [4] + rest, [2] + rest
    for even, odd in zip(even_bits, odd_bits):
        mine_sum = mine_sum + swap(mine_sum.astype(jnp.bfloat16), even, odd)
    first = mine_sum.astype(jnp.bfloat16)
    second, second_sibling = swap(first, 2, 4), swap(first, 3, 5)

    def products(outside, pieces, count, dtype, name, *got):
        return pl.pallas_call(
            functools.partial(section_kernel, near if got else 0),
            out_shape=jax.ShapeDtypeStruct((count, half, rows), dtype),
            in_specs=[vmem] * (4 + len(got)),
            out_specs=vmem,
            compiler_params=params,
            cost_estimate=pl.CostEstimate(
                flops=rows * variants * half * sections, bytes_accessed=rows * variants * 2, transcendentals=0
            ),
            name=name,
        )(outside, standard, *pieces, *got)

    def swap_chrom(x, bit):
        return lax.ppermute(x, "chrom", [(i, i ^ bit) for i in range(n_chrom)])

    bit = n_chrom // 2
    for_others = lambda pieces: products(outside_others, pieces, near + 1, jnp.bfloat16, "others")
    head = (first, swap(first, 1, 1))
    products_head = for_others(head)
    tail = (second, second_sibling)
    gots = [swap_chrom(products_head, bit), swap_chrom(for_others(tail), bit)]
    for_own = lambda pieces, *got: products(outside_own, pieces, sections // 2, jnp.float32, "own", *got)
    if n_chrom == 2:
        owns = [for_own(head, gots[0]), for_own(tail)]
    else:
        owns = [for_own(head), for_own(tail)]
        side = (lax.axis_index("chrom") // bit) % 2
        places = [received(c, sections, near, side) for c in range(sections // 2)]
        gots = [jnp.stack([lax.dynamic_index_in_dim(got, p, 0, False) for p in places]) for got in gots]
    while bit > 1:
        bit //= 2
        count = owns[0].shape[0] // 2
        side = (lax.axis_index("chrom") // bit) % 2
        sums = [own + got for own, got in zip(owns, gots)]
        gots = [
            swap_chrom(lax.dynamic_slice_in_dim(s, (1 - side) * count, count, 0).astype(jnp.bfloat16), bit) for s in sums
        ]
        owns = [lax.dynamic_slice_in_dim(s, side * count, count, 0) for s in sums]
    if n_chrom > 2:
        owns[0] = owns[0] + gots[0]

    out = pl.pallas_call(
        functools.partial(finish_kernel, near if n_chrom == 2 else 0),
        out_shape=jax.ShapeDtypeStruct((per_device, rhs, rows), jnp.float32),
        in_specs=[vmem] * 5,
        out_specs=vmem,
        compiler_params=params,
        name="finish",
    )(inverse, ridged, *owns, gots[1])
    return jnp.transpose(out, (0, 2, 1))


def solution(mesh):
    return jax.shard_map(
        on_device,
        mesh=mesh,
        in_specs=(P("samp", "chrom"), P("chrom"), P(), P(), P("samp", None)),
        out_specs=P("chrom", "samp", None),
        check_vma=False,
    )
```

```python
import functools

import jax
import jax.numpy as jnp
from jax import lax
from jax.experimental import pallas as pl
from jax.experimental.pallas import tpu as pltpu
from jax.sharding import PartitionSpec as P

VMEM_LIMIT = 24 * 1024 * 1024
BLOCK = 512


def half_and_bits():
    samp = lax.axis_index("samp")
    half, bit = samp % 2, 2
    while bit < lax.axis_size("samp"):
        half, bit = half + (samp // bit) % 2, bit * 2
    half = half % 2
    y, z = (samp // 2) % 2, (samp // 4) % 2
    return half, jnp.where(half == 0, y, z), jnp.where(half == 0, z, y)


def piece_rows(rhs):
    which, mine, sibling = half_and_bits()
    half, quarter = rhs // 2, rhs // 4
    return [
        which * half + mine * quarter,
        (1 - which) * half + sibling * quarter,
        which * half + (1 - mine) * quarter,
        (1 - which) * half + (1 - sibling) * quarter,
    ]


def cross_kernel(blocks, geno_hbm, freq_hbm, dir_hbm, stand_ref, *refs):
    quarters, (geno, freq_ref, dir_ref, sems) = refs[:4], refs[4:]
    width = geno_hbm.shape[1] // blocks
    small = [
        pltpu.make_async_copy(freq_hbm, freq_ref, sems.at[blocks]),
        pltpu.make_async_copy(dir_hbm, dir_ref, sems.at[blocks + 1]),
    ]
    for copy in small:
        copy.start()
    copies = []
    for i in range(blocks):
        columns = pl.ds(i * width, width)
        copies.append(pltpu.make_async_copy(geno_hbm.at[:, columns], geno.at[:, columns], sems.at[i]))
        copies[-1].start()
    quarter = dir_ref.shape[0] // 4
    mine, sibling, sent, sibling_sent = piece_rows(dir_ref.shape[0])
    for copy in small:
        copy.wait()
    vector = jnp.concatenate(
        [dir_ref[pl.ds(pl.multiple_of(row, quarter), quarter), :] for row in (sibling_sent, sibling, sent, mine)], axis=0
    ).astype(jnp.bfloat16)
    for i in range(blocks):
        columns = pl.ds(i * width, width)
        doubled = 2.0 * freq_ref[:, columns]
        scale = lax.rsqrt(doubled * (1.0 - freq_ref[:, columns]))
        copies[i].wait()
        standard = ((geno[:, columns].astype(jnp.float32) - doubled) * scale).astype(jnp.bfloat16)
        stand_ref[:, columns] = standard
        crossed = jnp.dot(vector, standard, preferred_element_type=jnp.float32)
        for q, ref in enumerate(quarters):
            ref[:, columns] = crossed[q * quarter : (q + 1) * quarter].astype(ref.dtype)


def prepare_kernel(total, widths_ref, ridge_ref, dir_ref, others_ref, own_ref, inverse_ref, ridged_ref):
    sections = widths_ref.shape[0]
    _, rows, variants = own_ref.shape
    per_device = inverse_ref.shape[0]
    near = others_ref.shape[0]
    rhs = dir_ref.shape[0]
    chrom = lax.axis_index("chrom")
    side = (chrom // (lax.axis_size("chrom") // 2)) % 2
    var = chrom * variants + lax.broadcasted_iota(jnp.int32, (1, variants), 1)
    start = jnp.int32(0)
    for c in range(sections):
        end = start + widths_ref[c]
        outside = jnp.where((var < start) | (var >= end), 1.0, 0.0)
        outside = jnp.broadcast_to(outside, (rows, variants)).astype(jnp.bfloat16)
        here = side == (0 if c < sections // 2 else 1)

        @pl.when(here)
        def _():
            own_ref[c % (sections // 2)] = outside

        if sections // 2 - near <= c < sections // 2 + near:

            @pl.when(jnp.logical_not(here))
            def _():
                others_ref[c - (sections // 2 - near if c < sections // 2 else sections // 2)] = outside

        start = end
    for c in range(per_device):
        divisor = (total - widths_ref[chrom * per_device + c]).astype(jnp.float32)
        inverse_ref[c] = 1.0 / jnp.full(inverse_ref.shape[1:], divisor, jnp.float32)
    for p, row in enumerate(piece_rows(rhs)):
        quarter = rhs // 4
        ridged_ref[pl.ds(p * quarter, quarter), :] = ridge_ref[0] * dir_ref[pl.ds(pl.multiple_of(row, quarter), quarter), :]


def received(c, sections, near, side):
    if sections // 2 <= near:
        return c + 1
    low = c - (sections // 2 - near) + 1
    return jnp.where(side == 0, max(low, 0), c + 1 if c < near else 0)


def section_kernel(near, outside_ref, stand_ref, *refs):
    pieces, got_ref, out_ref = refs[:2], refs[2], refs[-1]
    count = outside_ref.shape[0]
    spread = [p[...] for p in pieces] if out_ref.shape[0] > count else []
    spread += [p[...] * outside_ref[c] for c in range(count) for p in pieces]
    product = lax.dot_general(
        jnp.concatenate(spread, axis=0), stand_ref[...], (((1,), (1,)), ((), ())), preferred_element_type=jnp.float32
    )
    product = product.reshape(out_ref.shape)
    if not near:
        out_ref[...] = product.astype(out_ref.dtype)
        return
    side = lax.axis_index("chrom")
    for c in range(count):
        out_ref[c] = product[c] + got_ref[received(c, 2 * count, near, side)].astype(jnp.float32)


def finish_kernel(near, inverse_ref, ridged_ref, *refs):
    head_ref, tail_ref, got_ref, out_ref = refs
    per_device, rhs, _ = out_ref.shape
    side = lax.axis_index("chrom")
    places = [received(c, 2 * per_device, near, side) if near else c for c in range(per_device)]
    quarter = rhs // 4
    for p, row in enumerate(piece_rows(rhs)):
        at = pl.ds(pl.multiple_of(row, quarter), quarter)
        ridged = ridged_ref[pl.ds(p * quarter, quarter), :]
        here = pl.ds((p % 2) * quarter, quarter)
        for c in range(per_device):
            if p < 2:
                rest = head_ref[c, here, :]
            else:
                rest = tail_ref[c, here, :] + got_ref[places[c], here, :].astype(jnp.float32)
            out_ref[c, at, :] = ridged + rest * inverse_ref[c]


def on_device(genotypes, frequency, widths, ridge_term, direction):
    rows, variants = genotypes.shape
    rhs = direction.shape[1]
    sections = widths.shape[0]
    n_samp, n_chrom = lax.axis_size("samp"), lax.axis_size("chrom")
    per_device = sections // n_chrom
    half, quarter = rhs // 2, rhs // 4
    vmem = pl.BlockSpec(memory_space=pltpu.VMEM)
    smem = pl.BlockSpec(memory_space=pltpu.SMEM)
    params = pltpu.CompilerParams(vmem_limit_bytes=VMEM_LIMIT)
    dir_t = direction.T

    blocks = max(1, variants // BLOCK)
    operands = (genotypes, frequency.reshape(1, variants), dir_t)
    parts = [jax.ShapeDtypeStruct((quarter, variants), dtype) for dtype in (jnp.bfloat16, jnp.float32)]
    standard, give_first, give_second, keep_first, keep_second = pl.pallas_call(
        functools.partial(cross_kernel, blocks),
        out_shape=(
            jax.ShapeDtypeStruct((rows, variants), jnp.bfloat16),
            *(parts[i] for i in (0, 0, 1, 1)),
        ),
        in_specs=[pl.BlockSpec(memory_space=pl.ANY)] * 3,
        out_specs=(vmem,) * 5,
        scratch_shapes=[
            pltpu.VMEM((rows, variants), jnp.int32),
            pltpu.VMEM((1, variants), jnp.float32),
            pltpu.VMEM((rhs, rows), jnp.float32),
            pltpu.SemaphoreType.DMA((blocks + 2,)),
        ],
        compiler_params=params,
        name="cross",
    )(*(pltpu.with_memory_space_constraint(a, pltpu.HBM) for a in operands))

    near = max(1, sections // 4)
    mask = lambda count: jax.ShapeDtypeStruct((count, quarter, variants), jnp.bfloat16)
    outside_others, outside_own, inverse, ridged = pl.pallas_call(
        functools.partial(prepare_kernel, variants * n_chrom),
        out_shape=(
            mask(near),
            mask(sections // 2),
            jax.ShapeDtypeStruct((per_device, quarter, rows), jnp.float32),
            jax.ShapeDtypeStruct((rhs, rows), jnp.float32),
        ),
        in_specs=[smem, smem, vmem],
        out_specs=(vmem,) * 4,
        compiler_params=params,
        name="prepare",
    )(widths, ridge_term, dir_t)

    def swap(x, low, high):
        return lax.ppermute(x, "samp", [(i, i ^ (high if i.bit_count() % 2 else low)) for i in range(n_samp)])

    sent = (keep_first + swap(give_first, 1, 1)).astype(jnp.bfloat16)
    mine_sum = keep_second + swap(give_second, 1, 1) + swap(sent, 3, 5)
    mine_sum, outside_others, outside_own, inverse, ridged = lax.optimization_barrier(
        (mine_sum, outside_others, outside_own, inverse, ridged)
    )
    rest = [1 << b for b in range(3, n_samp.bit_length() - 1)]
    low_bits, high_bits = rest + [4], [2] + rest
    for low, high in zip(low_bits, high_bits):
        mine_sum = mine_sum + swap(mine_sum.astype(jnp.bfloat16), low | 1, high | 1)
    first = mine_sum.astype(jnp.bfloat16)
    second, second_sibling = swap(first, 3, 5), swap(first, 2, 4)

    def products(outside, pieces, count, dtype, name, *got):
        return pl.pallas_call(
            functools.partial(section_kernel, near if got else 0),
            out_shape=jax.ShapeDtypeStruct((count, half, rows), dtype),
            in_specs=[vmem] * (4 + len(got)),
            out_specs=vmem,
            compiler_params=params,
            cost_estimate=pl.CostEstimate(
                flops=rows * variants * half * sections, bytes_accessed=rows * variants * 2, transcendentals=0
            ),
            name=name,
        )(outside, standard, *pieces, *got)

    def swap_chrom(x, bit):
        return lax.ppermute(x, "chrom", [(i, i ^ bit) for i in range(n_chrom)])

    bit = n_chrom // 2
    for_others = lambda pieces: products(outside_others, pieces, near + 1, jnp.bfloat16, "others")
    head = (first, swap(first, 1, 1))
    products_head = for_others(head)
    tail = (second, second_sibling)
    gots = [swap_chrom(products_head, bit), swap_chrom(for_others(tail), bit)]
    for_own = lambda pieces, *got: products(outside_own, pieces, sections // 2, jnp.float32, "own", *got)
    if n_chrom == 2:
        owns = [for_own(head, gots[0]), for_own(tail)]
    else:
        owns = [for_own(head), for_own(tail)]
        side = (lax.axis_index("chrom") // bit) % 2
        places = [received(c, sections, near, side) for c in range(sections // 2)]
        gots = [jnp.stack([lax.dynamic_index_in_dim(got, p, 0, False) for p in places]) for got in gots]
    while bit > 1:
        bit //= 2
        count = owns[0].shape[0] // 2
        side = (lax.axis_index("chrom") // bit) % 2
        sums = [own + got for own, got in zip(owns, gots)]
        gots = [
            swap_chrom(lax.dynamic_slice_in_dim(s, (1 - side) * count, count, 0).astype(jnp.bfloat16), bit) for s in sums
        ]
        owns = [lax.dynamic_slice_in_dim(s, side * count, count, 0) for s in sums]
    if n_chrom > 2:
        owns[0] = owns[0] + gots[0]

    out = pl.pallas_call(
        functools.partial(finish_kernel, near if n_chrom == 2 else 0),
        out_shape=jax.ShapeDtypeStruct((per_device, rhs, rows), jnp.float32),
        in_specs=[vmem] * 5,
        out_specs=vmem,
        compiler_params=params,
        name="finish",
    )(inverse, ridged, *owns, gots[1])
    return jnp.transpose(out, (0, 2, 1))


def solution(mesh):
    return jax.shard_map(
        on_device,
        mesh=mesh,
        in_specs=(P("samp", "chrom"), P("chrom"), P(), P(), P("samp", None)),
        out_specs=P("chrom", "samp", None),
        check_vma=False,
    )
```

```python
import functools

import jax
import jax.numpy as jnp
from jax import lax
from jax.experimental import pallas as pl
from jax.experimental.pallas import tpu as pltpu
from jax.sharding import PartitionSpec as P

VMEM_LIMIT = 24 * 1024 * 1024
BLOCK = 512


def half_and_bits():
    samp = lax.axis_index("samp")
    half, bit = samp % 2, 2
    while bit < lax.axis_size("samp"):
        half, bit = half + (samp // bit) % 2, bit * 2
    half = half % 2
    y, z = (samp // 2) % 2, (samp // 4) % 2
    return half, jnp.where(half == 0, y, z), jnp.where(half == 0, z, y)


def piece_rows(rhs):
    which, mine, sibling = half_and_bits()
    half, quarter = rhs // 2, rhs // 4
    return [
        which * half + mine * quarter,
        (1 - which) * half + sibling * quarter,
        which * half + (1 - mine) * quarter,
        (1 - which) * half + (1 - sibling) * quarter,
    ]


def cross_kernel(blocks, geno_hbm, freq_hbm, dir_hbm, stand_ref, *refs):
    quarters, (geno, freq_ref, dir_ref, sems) = refs[:4], refs[4:]
    width = geno_hbm.shape[1] // blocks
    small = [
        pltpu.make_async_copy(freq_hbm, freq_ref, sems.at[blocks]),
        pltpu.make_async_copy(dir_hbm, dir_ref, sems.at[blocks + 1]),
    ]
    for copy in small:
        copy.start()
    copies = []
    for i in range(blocks):
        columns = pl.ds(i * width, width)
        copies.append(pltpu.make_async_copy(geno_hbm.at[:, columns], geno.at[:, columns], sems.at[i]))
        copies[-1].start()
    quarter = dir_ref.shape[0] // 4
    mine, sibling, sent, sibling_sent = piece_rows(dir_ref.shape[0])
    for copy in small:
        copy.wait()
    vector = jnp.concatenate(
        [dir_ref[pl.ds(pl.multiple_of(row, quarter), quarter), :] for row in (sibling_sent, sibling, sent, mine)], axis=0
    ).astype(jnp.bfloat16)
    for i in range(blocks):
        columns = pl.ds(i * width, width)
        doubled = 2.0 * freq_ref[:, columns]
        scale = lax.rsqrt(doubled * (1.0 - freq_ref[:, columns]))
        copies[i].wait()
        standard = ((geno[:, columns].astype(jnp.float32) - doubled) * scale).astype(jnp.bfloat16)
        stand_ref[:, columns] = standard
        crossed = jnp.dot(vector, standard, preferred_element_type=jnp.float32)
        for q, ref in enumerate(quarters):
            ref[:, columns] = crossed[q * quarter : (q + 1) * quarter].astype(ref.dtype)


def prepare_kernel(total, widths_ref, ridge_ref, dir_ref, others_ref, own_ref, inverse_ref, ridged_ref):
    sections = widths_ref.shape[0]
    _, rows, variants = own_ref.shape
    per_device = inverse_ref.shape[0]
    near = others_ref.shape[0]
    rhs = dir_ref.shape[0]
    chrom = lax.axis_index("chrom")
    side = (chrom // (lax.axis_size("chrom") // 2)) % 2
    var = chrom * variants + lax.broadcasted_iota(jnp.int32, (1, variants), 1)
    start = jnp.int32(0)
    for c in range(sections):
        end = start + widths_ref[c]
        outside = jnp.where((var < start) | (var >= end), 1.0, 0.0)
        outside = jnp.broadcast_to(outside, (rows, variants)).astype(jnp.bfloat16)
        here = side == (0 if c < sections // 2 else 1)

        @pl.when(here)
        def _():
            own_ref[c % (sections // 2)] = outside

        if sections // 2 - near <= c < sections // 2 + near:

            @pl.when(jnp.logical_not(here))
            def _():
                others_ref[c - (sections // 2 - near if c < sections // 2 else sections // 2)] = outside

        start = end
    for c in range(per_device):
        divisor = (total - widths_ref[chrom * per_device + c]).astype(jnp.float32)
        inverse_ref[c] = 1.0 / jnp.full(inverse_ref.shape[1:], divisor, jnp.float32)
    for p, row in enumerate(piece_rows(rhs)):
        quarter = rhs // 4
        ridged_ref[pl.ds(p * quarter, quarter), :] = ridge_ref[0] * dir_ref[pl.ds(pl.multiple_of(row, quarter), quarter), :]


def received(c, sections, near, side):
    if sections // 2 <= near:
        return c + 1
    low = c - (sections // 2 - near) + 1
    return jnp.where(side == 0, max(low, 0), c + 1 if c < near else 0)


def turn_kernel(stand_ref, turned_ref):
    turned_ref[...] = stand_ref[...].T


def section_kernel(near, outside_ref, turned_ref, *refs):
    pieces, got_ref, out_ref = refs[:2], refs[2], refs[-1]
    count = outside_ref.shape[0]
    spread = [p[...] for p in pieces] if out_ref.shape[0] > count else []
    spread += [p[...] * outside_ref[c] for c in range(count) for p in pieces]
    product = jnp.dot(jnp.concatenate(spread, axis=0), turned_ref[...], preferred_element_type=jnp.float32)
    product = product.reshape(out_ref.shape)
    if not near:
        out_ref[...] = product.astype(out_ref.dtype)
        return
    side = lax.axis_index("chrom")
    for c in range(count):
        out_ref[c] = product[c] + got_ref[received(c, 2 * count, near, side)].astype(jnp.float32)


def finish_kernel(near, inverse_ref, ridged_ref, *refs):
    head_ref, tail_ref, got_ref, out_ref = refs
    per_device, rhs, _ = out_ref.shape
    side = lax.axis_index("chrom")
    places = [received(c, 2 * per_device, near, side) if near else c for c in range(per_device)]
    quarter = rhs // 4
    for p, row in enumerate(piece_rows(rhs)):
        at = pl.ds(pl.multiple_of(row, quarter), quarter)
        ridged = ridged_ref[pl.ds(p * quarter, quarter), :]
        here = pl.ds((p % 2) * quarter, quarter)
        for c in range(per_device):
            if p < 2:
                rest = head_ref[c, here, :]
            else:
                rest = tail_ref[c, here, :] + got_ref[places[c], here, :].astype(jnp.float32)
            out_ref[c, at, :] = ridged + rest * inverse_ref[c]


def on_device(genotypes, frequency, widths, ridge_term, direction):
    rows, variants = genotypes.shape
    rhs = direction.shape[1]
    sections = widths.shape[0]
    n_samp, n_chrom = lax.axis_size("samp"), lax.axis_size("chrom")
    per_device = sections // n_chrom
    half, quarter = rhs // 2, rhs // 4
    vmem = pl.BlockSpec(memory_space=pltpu.VMEM)
    smem = pl.BlockSpec(memory_space=pltpu.SMEM)
    params = pltpu.CompilerParams(vmem_limit_bytes=VMEM_LIMIT)
    dir_t = direction.T

    blocks = max(1, variants // BLOCK)
    operands = (genotypes, frequency.reshape(1, variants), dir_t)
    parts = [jax.ShapeDtypeStruct((quarter, variants), dtype) for dtype in (jnp.bfloat16, jnp.float32)]
    standard, give_first, give_second, keep_first, keep_second = pl.pallas_call(
        functools.partial(cross_kernel, blocks),
        out_shape=(
            jax.ShapeDtypeStruct((rows, variants), jnp.bfloat16),
            *(parts[i] for i in (0, 0, 1, 1)),
        ),
        in_specs=[pl.BlockSpec(memory_space=pl.ANY)] * 3,
        out_specs=(vmem,) * 5,
        scratch_shapes=[
            pltpu.VMEM((rows, variants), jnp.int32),
            pltpu.VMEM((1, variants), jnp.float32),
            pltpu.VMEM((rhs, rows), jnp.float32),
            pltpu.SemaphoreType.DMA((blocks + 2,)),
        ],
        compiler_params=params,
        name="cross",
    )(*(pltpu.with_memory_space_constraint(a, pltpu.HBM) for a in operands))

    near = max(1, sections // 4)
    mask = lambda count: jax.ShapeDtypeStruct((count, quarter, variants), jnp.bfloat16)
    outside_others, outside_own, inverse, ridged = pl.pallas_call(
        functools.partial(prepare_kernel, variants * n_chrom),
        out_shape=(
            mask(near),
            mask(sections // 2),
            jax.ShapeDtypeStruct((per_device, quarter, rows), jnp.float32),
            jax.ShapeDtypeStruct((rhs, rows), jnp.float32),
        ),
        in_specs=[smem, smem, vmem],
        out_specs=(vmem,) * 4,
        compiler_params=params,
        name="prepare",
    )(widths, ridge_term, dir_t)

    def swap(x, low, high):
        return lax.ppermute(x, "samp", [(i, i ^ (high if i.bit_count() % 2 else low)) for i in range(n_samp)])

    sent = (keep_first + swap(give_first, 1, 1)).astype(jnp.bfloat16)
    mine_sum = keep_second + swap(give_second, 1, 1) + swap(sent, 3, 5)
    mine_sum, outside_others, outside_own, inverse, ridged = lax.optimization_barrier(
        (mine_sum, outside_others, outside_own, inverse, ridged)
    )
    rest = [1 << b for b in range(3, n_samp.bit_length() - 1)]
    low_bits, high_bits = rest + [4], [2] + rest
    turned = pl.pallas_call(
        turn_kernel,
        out_shape=jax.ShapeDtypeStruct((variants, rows), jnp.bfloat16),
        in_specs=[vmem],
        out_specs=vmem,
        compiler_params=params,
        name="turn",
    )(standard)
    for step, (low, high) in enumerate(zip(low_bits, high_bits)):
        mine_sum = mine_sum + swap(mine_sum.astype(jnp.bfloat16), low | 1, high | 1)
        if step == 0:
            mine_sum, turned = lax.optimization_barrier((mine_sum, turned))
    first = mine_sum.astype(jnp.bfloat16)
    second, second_sibling = swap(first, 3, 5), swap(first, 2, 4)

    def products(outside, pieces, count, dtype, name, *got):
        return pl.pallas_call(
            functools.partial(section_kernel, near if got else 0),
            out_shape=jax.ShapeDtypeStruct((count, half, rows), dtype),
            in_specs=[vmem] * (4 + len(got)),
            out_specs=vmem,
            compiler_params=params,
            cost_estimate=pl.CostEstimate(
                flops=rows * variants * half * sections, bytes_accessed=rows * variants * 2, transcendentals=0
            ),
            name=name,
        )(outside, turned, *pieces, *got)

    def swap_chrom(x, bit):
        return lax.ppermute(x, "chrom", [(i, i ^ bit) for i in range(n_chrom)])

    bit = n_chrom // 2
    for_others = lambda pieces: products(outside_others, pieces, near + 1, jnp.bfloat16, "others")
    head = (first, swap(first, 1, 1))
    products_head = for_others(head)
    tail = (second, second_sibling)
    gots = [swap_chrom(products_head, bit), swap_chrom(for_others(tail), bit)]
    for_own = lambda pieces, *got: products(outside_own, pieces, sections // 2, jnp.float32, "own", *got)
    if n_chrom == 2:
        owns = [for_own(head, gots[0]), for_own(tail)]
    else:
        owns = [for_own(head), for_own(tail)]
        side = (lax.axis_index("chrom") // bit) % 2
        places = [received(c, sections, near, side) for c in range(sections // 2)]
        gots = [jnp.stack([lax.dynamic_index_in_dim(got, p, 0, False) for p in places]) for got in gots]
    while bit > 1:
        bit //= 2
        count = owns[0].shape[0] // 2
        side = (lax.axis_index("chrom") // bit) % 2
        sums = [own + got for own, got in zip(owns, gots)]
        gots = [
            swap_chrom(lax.dynamic_slice_in_dim(s, (1 - side) * count, count, 0).astype(jnp.bfloat16), bit) for s in sums
        ]
        owns = [lax.dynamic_slice_in_dim(s, side * count, count, 0) for s in sums]
    if n_chrom > 2:
        owns[0] = owns[0] + gots[0]

    out = pl.pallas_call(
        functools.partial(finish_kernel, near if n_chrom == 2 else 0),
        out_shape=jax.ShapeDtypeStruct((per_device, rhs, rows), jnp.float32),
        in_specs=[vmem] * 5,
        out_specs=vmem,
        compiler_params=params,
        name="finish",
    )(inverse, ridged, *owns, gots[1])
    return jnp.transpose(out, (0, 2, 1))


def solution(mesh):
    return jax.shard_map(
        on_device,
        mesh=mesh,
        in_specs=(P("samp", "chrom"), P("chrom"), P(), P(), P("samp", None)),
        out_specs=P("chrom", "samp", None),
        check_vma=False,
    )
```

```python
import functools

import jax
import jax.numpy as jnp
from jax import lax
from jax.experimental import pallas as pl
from jax.experimental.pallas import tpu as pltpu
from jax.sharding import PartitionSpec as P

VMEM_LIMIT = 24 * 1024 * 1024
BLOCK = 512


def half_and_bits():
    samp = lax.axis_index("samp")
    half, bit = samp % 2, 2
    while bit < lax.axis_size("samp"):
        half, bit = half + (samp // bit) % 2, bit * 2
    half = half % 2
    y, z = (samp // 2) % 2, (samp // 4) % 2
    return half, jnp.where(half == 0, y, z), jnp.where(half == 0, z, y)


def piece_rows(rhs):
    which, mine, sibling = half_and_bits()
    half, quarter = rhs // 2, rhs // 4
    return [
        which * half + mine * quarter,
        (1 - which) * half + sibling * quarter,
        which * half + (1 - mine) * quarter,
        (1 - which) * half + (1 - sibling) * quarter,
    ]


def cross_kernel(blocks, geno_hbm, freq_hbm, dir_hbm, stand_ref, *refs):
    quarters, (geno, freq_ref, dir_ref, sems) = refs[:4], refs[4:]
    width = geno_hbm.shape[1] // blocks
    small = [
        pltpu.make_async_copy(freq_hbm, freq_ref, sems.at[blocks]),
        pltpu.make_async_copy(dir_hbm, dir_ref, sems.at[blocks + 1]),
    ]
    for copy in small:
        copy.start()
    copies = []
    for i in range(blocks):
        columns = pl.ds(i * width, width)
        copies.append(pltpu.make_async_copy(geno_hbm.at[:, columns], geno.at[:, columns], sems.at[i]))
        copies[-1].start()
    quarter = dir_ref.shape[0] // 4
    mine, sibling, sent, sibling_sent = piece_rows(dir_ref.shape[0])
    for copy in small:
        copy.wait()
    vector = jnp.concatenate(
        [dir_ref[pl.ds(pl.multiple_of(row, quarter), quarter), :] for row in (sibling_sent, sibling, sent, mine)], axis=0
    ).astype(jnp.bfloat16)
    for i in range(blocks):
        columns = pl.ds(i * width, width)
        doubled = 2.0 * freq_ref[:, columns]
        scale = lax.rsqrt(doubled * (1.0 - freq_ref[:, columns]))
        copies[i].wait()
        standard = ((geno[:, columns].astype(jnp.float32) - doubled) * scale).astype(jnp.bfloat16)
        stand_ref[:, columns] = standard
        crossed = jnp.dot(vector, standard, preferred_element_type=jnp.float32)
        for q, ref in enumerate(quarters):
            ref[:, columns] = crossed[q * quarter : (q + 1) * quarter].astype(ref.dtype)


def prepare_kernel(total, widths_ref, ridge_ref, dir_ref, others_ref, own_ref, inverse_ref, ridged_ref):
    sections = widths_ref.shape[0]
    _, rows, variants = own_ref.shape
    per_device = inverse_ref.shape[0]
    near = others_ref.shape[0]
    rhs = dir_ref.shape[0]
    chrom = lax.axis_index("chrom")
    side = (chrom // (lax.axis_size("chrom") // 2)) % 2
    var = chrom * variants + lax.broadcasted_iota(jnp.int32, (1, variants), 1)
    start = jnp.int32(0)
    for c in range(sections):
        end = start + widths_ref[c]
        outside = jnp.where((var < start) | (var >= end), 1.0, 0.0)
        outside = jnp.broadcast_to(outside, (rows, variants)).astype(jnp.bfloat16)
        here = side == (0 if c < sections // 2 else 1)

        @pl.when(here)
        def _():
            own_ref[c % (sections // 2)] = outside

        if sections // 2 - near <= c < sections // 2 + near:

            @pl.when(jnp.logical_not(here))
            def _():
                others_ref[c - (sections // 2 - near if c < sections // 2 else sections // 2)] = outside

        start = end
    for c in range(per_device):
        divisor = (total - widths_ref[chrom * per_device + c]).astype(jnp.float32)
        inverse_ref[c] = 1.0 / jnp.full(inverse_ref.shape[1:], divisor, jnp.float32)
    for p, row in enumerate(piece_rows(rhs)):
        quarter = rhs // 4
        ridged_ref[pl.ds(p * quarter, quarter), :] = ridge_ref[0] * dir_ref[pl.ds(pl.multiple_of(row, quarter), quarter), :]


def received(c, sections, near, side):
    if sections // 2 <= near:
        return c + 1
    low = c - (sections // 2 - near) + 1
    return jnp.where(side == 0, max(low, 0), c + 1 if c < near else 0)


def turn_kernel(stand_ref, turned_ref):
    turned_ref[...] = stand_ref[...].T


def section_kernel(near, outside_ref, turned_ref, *refs):
    pieces, got_ref, out_ref = refs[:2], refs[2], refs[-1]
    count = outside_ref.shape[0]
    spread = [p[...] for p in pieces] if out_ref.shape[0] > count else []
    spread += [p[...] * outside_ref[c] for c in range(count) for p in pieces]
    product = jnp.dot(jnp.concatenate(spread, axis=0), turned_ref[...], preferred_element_type=jnp.float32)
    product = product.reshape(out_ref.shape)
    if not near:
        out_ref[...] = product.astype(out_ref.dtype)
        return
    side = lax.axis_index("chrom")
    for c in range(count):
        out_ref[c] = product[c] + got_ref[received(c, 2 * count, near, side)].astype(jnp.float32)


def finish_kernel(near, group, inverse_ref, ridged_ref, own_ref, *refs):
    out_hbm, done, sems = refs[-3:]
    got = refs[:-3]
    per_device, rhs, _ = out_hbm.shape
    side = lax.axis_index("chrom")
    places = [received(c, 2 * per_device, near, side) if near else c for c in range(per_device)]
    quarter = rhs // 4
    rows = piece_rows(rhs)[2 * group : 2 * group + 2]
    copies = []
    for p, row in enumerate(rows):
        here = pl.ds(p * quarter, quarter)
        ridged = ridged_ref[pl.ds((2 * group + p) * quarter, quarter), :]
        for c in range(per_device):
            rest = own_ref[c, here, :]
            if group == 1:
                rest = rest + got[0][places[c], here, :].astype(jnp.float32)
            done[p, c] = ridged + rest * inverse_ref[c]
        to = out_hbm.at[:, pl.ds(pl.multiple_of(row, quarter), quarter), :]
        copies.append(pltpu.make_async_copy(done.at[p], to, sems.at[p]))
        copies[-1].start()
    for copy in copies:
        copy.wait()


def on_device(genotypes, frequency, widths, ridge_term, direction):
    rows, variants = genotypes.shape
    rhs = direction.shape[1]
    sections = widths.shape[0]
    n_samp, n_chrom = lax.axis_size("samp"), lax.axis_size("chrom")
    per_device = sections // n_chrom
    half, quarter = rhs // 2, rhs // 4
    vmem = pl.BlockSpec(memory_space=pltpu.VMEM)
    smem = pl.BlockSpec(memory_space=pltpu.SMEM)
    anywhere = pl.BlockSpec(memory_space=pl.ANY)
    params = pltpu.CompilerParams(vmem_limit_bytes=VMEM_LIMIT)
    dir_t = direction.T

    blocks = max(1, variants // BLOCK)
    operands = (genotypes, frequency.reshape(1, variants), dir_t)
    parts = [jax.ShapeDtypeStruct((quarter, variants), dtype) for dtype in (jnp.bfloat16, jnp.float32)]
    standard, give_first, give_second, keep_first, keep_second = pl.pallas_call(
        functools.partial(cross_kernel, blocks),
        out_shape=(
            jax.ShapeDtypeStruct((rows, variants), jnp.bfloat16),
            *(parts[i] for i in (0, 0, 1, 1)),
        ),
        in_specs=[pl.BlockSpec(memory_space=pl.ANY)] * 3,
        out_specs=(vmem,) * 5,
        scratch_shapes=[
            pltpu.VMEM((rows, variants), jnp.int32),
            pltpu.VMEM((1, variants), jnp.float32),
            pltpu.VMEM((rhs, rows), jnp.float32),
            pltpu.SemaphoreType.DMA((blocks + 2,)),
        ],
        compiler_params=params,
        name="cross",
    )(*(pltpu.with_memory_space_constraint(a, pltpu.HBM) for a in operands))

    near = max(1, sections // 2 - 2)
    mask = lambda count: jax.ShapeDtypeStruct((count, quarter, variants), jnp.bfloat16)
    outside_others, outside_own, inverse, ridged = pl.pallas_call(
        functools.partial(prepare_kernel, variants * n_chrom),
        out_shape=(
            mask(near),
            mask(sections // 2),
            jax.ShapeDtypeStruct((per_device, quarter, rows), jnp.float32),
            jax.ShapeDtypeStruct((rhs, rows), jnp.float32),
        ),
        in_specs=[smem, smem, vmem],
        out_specs=(vmem,) * 4,
        compiler_params=params,
        name="prepare",
    )(widths, ridge_term, dir_t)

    def swap(x, low, high):
        return lax.ppermute(x, "samp", [(i, i ^ (high if i.bit_count() % 2 else low)) for i in range(n_samp)])

    sent = (keep_first + swap(give_first, 1, 1)).astype(jnp.bfloat16)
    mine_sum = keep_second + swap(give_second, 1, 1) + swap(sent, 3, 5)
    mine_sum, outside_others, outside_own, inverse, ridged = lax.optimization_barrier(
        (mine_sum, outside_others, outside_own, inverse, ridged)
    )
    rest = [1 << b for b in range(3, n_samp.bit_length() - 1)]
    low_bits, high_bits = rest + [4], [2] + rest
    turned = pl.pallas_call(
        turn_kernel,
        out_shape=jax.ShapeDtypeStruct((variants, rows), jnp.bfloat16),
        in_specs=[vmem],
        out_specs=vmem,
        compiler_params=params,
        name="turn",
    )(standard)
    for step, (low, high) in enumerate(zip(low_bits, high_bits)):
        mine_sum = mine_sum + swap(mine_sum.astype(jnp.bfloat16), low | 1, high | 1)
        if step == 0:
            mine_sum, turned = lax.optimization_barrier((mine_sum, turned))
    first = mine_sum.astype(jnp.bfloat16)
    second, second_sibling = swap(first, 3, 5), swap(first, 2, 4)

    def products(outside, pieces, count, dtype, name, *got):
        return pl.pallas_call(
            functools.partial(section_kernel, near if got else 0),
            out_shape=jax.ShapeDtypeStruct((count, half, rows), dtype),
            in_specs=[vmem] * (4 + len(got)),
            out_specs=vmem,
            compiler_params=params,
            cost_estimate=pl.CostEstimate(
                flops=rows * variants * half * sections, bytes_accessed=rows * variants * 2, transcendentals=0
            ),
            name=name,
        )(outside, turned, *pieces, *got)

    def swap_chrom(x, bit):
        return lax.ppermute(x, "chrom", [(i, i ^ bit) for i in range(n_chrom)])

    bit = n_chrom // 2
    for_others = lambda pieces: products(outside_others, pieces, near + 1, jnp.bfloat16, "others")
    head = (first, swap(first, 1, 1))
    products_head = for_others(head)
    tail = (second, second_sibling)
    gots = [swap_chrom(products_head, bit), swap_chrom(for_others(tail), bit)]
    for_own = lambda pieces, *got: products(outside_own, pieces, sections // 2, jnp.float32, "own", *got)
    if n_chrom == 2:
        owns = [for_own(head, gots[0]), for_own(tail)]
    else:
        owns = [for_own(head), for_own(tail)]
        side = (lax.axis_index("chrom") // bit) % 2
        places = [received(c, sections, near, side) for c in range(sections // 2)]
        gots = [jnp.stack([lax.dynamic_index_in_dim(got, p, 0, False) for p in places]) for got in gots]
    while bit > 1:
        bit //= 2
        count = owns[0].shape[0] // 2
        side = (lax.axis_index("chrom") // bit) % 2
        sums = [own + got for own, got in zip(owns, gots)]
        gots = [
            swap_chrom(lax.dynamic_slice_in_dim(s, (1 - side) * count, count, 0).astype(jnp.bfloat16), bit) for s in sums
        ]
        owns = [lax.dynamic_slice_in_dim(s, side * count, count, 0) for s in sums]
    if n_chrom > 2:
        owns[0] = owns[0] + gots[0]

    def finish(group, *operands):
        return pl.pallas_call(
            functools.partial(finish_kernel, near if n_chrom == 2 else 0, group),
            out_shape=jax.ShapeDtypeStruct((per_device, rhs, rows), jnp.float32),
            in_specs=[vmem] * (3 + group) + [anywhere] * group,
            out_specs=anywhere,
            scratch_shapes=[
                pltpu.VMEM((2, per_device, quarter, rows), jnp.float32),
                pltpu.SemaphoreType.DMA((2,)),
            ],
            input_output_aliases={4: 0} if group else {},
            compiler_params=params,
            name="finish",
        )(inverse, ridged, *operands)

    out = pltpu.with_memory_space_constraint(finish(0, owns[0]), pltpu.HBM)
    out = finish(1, owns[1], gots[1], out)
    return jnp.transpose(out, (0, 2, 1))


def solution(mesh):
    return jax.shard_map(
        on_device,
        mesh=mesh,
        in_specs=(P("samp", "chrom"), P("chrom"), P(), P(), P("samp", None)),
        out_specs=P("chrom", "samp", None),
        check_vma=False,
    )
```

```python
import functools

import jax
import jax.numpy as jnp
from jax import lax
from jax.experimental import pallas as pl
from jax.experimental.pallas import tpu as pltpu
from jax.sharding import PartitionSpec as P

VMEM_LIMIT = 24 * 1024 * 1024
BLOCK = 512


def half_and_bits():
    samp = lax.axis_index("samp")
    half, bit = samp % 2, 2
    while bit < lax.axis_size("samp"):
        half, bit = half + (samp // bit) % 2, bit * 2
    half = half % 2
    y, z = (samp // 2) % 2, (samp // 4) % 2
    return half, jnp.where(half == 0, y, z), jnp.where(half == 0, z, y)


def piece_rows(rhs):
    which, mine, sibling = half_and_bits()
    half, quarter = rhs // 2, rhs // 4
    return [
        which * half + mine * quarter,
        (1 - which) * half + sibling * quarter,
        which * half + (1 - mine) * quarter,
        (1 - which) * half + (1 - sibling) * quarter,
    ]


def cross_kernel(blocks, geno_hbm, freq_hbm, dir_hbm, stand_ref, *refs):
    quarters, (geno, freq_ref, dir_ref, sems) = refs[:4], refs[4:]
    width = geno_hbm.shape[1] // blocks
    small = [
        pltpu.make_async_copy(freq_hbm, freq_ref, sems.at[blocks]),
        pltpu.make_async_copy(dir_hbm, dir_ref, sems.at[blocks + 1]),
    ]
    for copy in small:
        copy.start()
    copies = []
    for i in range(blocks):
        columns = pl.ds(i * width, width)
        copies.append(pltpu.make_async_copy(geno_hbm.at[:, columns], geno.at[:, columns], sems.at[i]))
        copies[-1].start()
    quarter = dir_ref.shape[0] // 4
    mine, sibling, sent, sibling_sent = piece_rows(dir_ref.shape[0])
    for copy in small:
        copy.wait()
    vector = jnp.concatenate(
        [dir_ref[pl.ds(pl.multiple_of(row, quarter), quarter), :] for row in (sibling_sent, sibling, sent, mine)], axis=0
    ).astype(jnp.bfloat16)
    for i in range(blocks):
        columns = pl.ds(i * width, width)
        doubled = 2.0 * freq_ref[:, columns]
        scale = lax.rsqrt(doubled * (1.0 - freq_ref[:, columns]))
        copies[i].wait()
        standard = ((geno[:, columns].astype(jnp.float32) - doubled) * scale).astype(jnp.bfloat16)
        stand_ref[:, columns] = standard
        crossed = jnp.dot(vector, standard, preferred_element_type=jnp.float32)
        for q, ref in enumerate(quarters):
            ref[:, columns] = crossed[q * quarter : (q + 1) * quarter].astype(ref.dtype)


def prepare_kernel(total, widths_ref, ridge_ref, dir_ref, others_ref, own_ref, inverse_ref, ridged_ref):
    sections = widths_ref.shape[0]
    _, rows, variants = own_ref.shape
    per_device = inverse_ref.shape[0]
    near = others_ref.shape[0]
    rhs = dir_ref.shape[0]
    chrom = lax.axis_index("chrom")
    side = (chrom // (lax.axis_size("chrom") // 2)) % 2
    var = chrom * variants + lax.broadcasted_iota(jnp.int32, (1, variants), 1)
    start = jnp.int32(0)
    for c in range(sections):
        end = start + widths_ref[c]
        outside = jnp.where((var < start) | (var >= end), 1.0, 0.0)
        outside = jnp.broadcast_to(outside, (rows, variants)).astype(jnp.bfloat16)
        here = side == (0 if c < sections // 2 else 1)

        @pl.when(here)
        def _():
            own_ref[c % (sections // 2)] = outside

        if sections // 2 - near <= c < sections // 2 + near:

            @pl.when(jnp.logical_not(here))
            def _():
                others_ref[c - (sections // 2 - near if c < sections // 2 else sections // 2)] = outside

        start = end
    for c in range(per_device):
        divisor = (total - widths_ref[chrom * per_device + c]).astype(jnp.float32)
        inverse_ref[c] = 1.0 / jnp.full(inverse_ref.shape[1:], divisor, jnp.float32)
    for p, row in enumerate(piece_rows(rhs)):
        quarter = rhs // 4
        ridged_ref[pl.ds(p * quarter, quarter), :] = ridge_ref[0] * dir_ref[pl.ds(pl.multiple_of(row, quarter), quarter), :]


def received(c, sections, near, side):
    if sections // 2 <= near:
        return c + 1
    low = c - (sections // 2 - near) + 1
    return jnp.where(side == 0, max(low, 0), c + 1 if c < near else 0)


def turn_kernel(stand_ref, turned_ref):
    turned_ref[...] = stand_ref[...].T


def section_kernel(near, outside_ref, turned_ref, *refs):
    pieces, got_ref, out_ref = (refs[:-2] if near else refs[:-1]), refs[-2], refs[-1]
    count = outside_ref.shape[0]
    spread = [p[...] for p in pieces] if out_ref.shape[0] > count else []
    spread += [p[...] * outside_ref[c] for c in range(count) for p in pieces]
    product = jnp.dot(jnp.concatenate(spread, axis=0), turned_ref[...], preferred_element_type=jnp.float32)
    product = product.reshape(out_ref.shape)
    if not near:
        out_ref[...] = product.astype(out_ref.dtype)
        return
    side = lax.axis_index("chrom")
    for c in range(count):
        out_ref[c] = product[c] + got_ref[received(c, 2 * count, near, side)].astype(jnp.float32)


def join_kernel(near, own_ref, got_ref, out_ref):
    count = own_ref.shape[0]
    side = lax.axis_index("chrom")
    for c in range(count):
        out_ref[c] = own_ref[c] + got_ref[received(c, 2 * count, near, side)].astype(jnp.float32)


def finish_kernel(near, inverse_ref, ridged_ref, head_ref, tail_ref, got_ref, out_ref):
    per_device, rhs, _ = out_ref.shape
    side = lax.axis_index("chrom")
    places = [received(c, 2 * per_device, near, side) if near else c for c in range(per_device)]
    quarter = rhs // 4
    for p, row in enumerate(piece_rows(rhs)):
        at = pl.ds(pl.multiple_of(row, quarter), quarter)
        ridged = ridged_ref[pl.ds(p * quarter, quarter), :]
        for c in range(per_device):
            if p == 2:
                rest = tail_ref[c] + got_ref[places[c]].astype(jnp.float32)
            else:
                rest = head_ref[c, pl.ds(min(p, 2) * quarter, quarter), :]
            out_ref[c, at, :] = ridged + rest * inverse_ref[c]


def on_device(genotypes, frequency, widths, ridge_term, direction):
    rows, variants = genotypes.shape
    rhs = direction.shape[1]
    sections = widths.shape[0]
    n_samp, n_chrom = lax.axis_size("samp"), lax.axis_size("chrom")
    per_device = sections // n_chrom
    half, quarter = rhs // 2, rhs // 4
    vmem = pl.BlockSpec(memory_space=pltpu.VMEM)
    smem = pl.BlockSpec(memory_space=pltpu.SMEM)
    anywhere = pl.BlockSpec(memory_space=pl.ANY)
    params = pltpu.CompilerParams(vmem_limit_bytes=VMEM_LIMIT)
    dir_t = direction.T

    blocks = max(1, variants // BLOCK)
    operands = (genotypes, frequency.reshape(1, variants), dir_t)
    parts = [jax.ShapeDtypeStruct((quarter, variants), dtype) for dtype in (jnp.bfloat16, jnp.float32)]
    standard, give_first, give_second, keep_first, keep_second = pl.pallas_call(
        functools.partial(cross_kernel, blocks),
        out_shape=(
            jax.ShapeDtypeStruct((rows, variants), jnp.bfloat16),
            *(parts[i] for i in (0, 0, 1, 1)),
        ),
        in_specs=[pl.BlockSpec(memory_space=pl.ANY)] * 3,
        out_specs=(vmem,) * 5,
        scratch_shapes=[
            pltpu.VMEM((rows, variants), jnp.int32),
            pltpu.VMEM((1, variants), jnp.float32),
            pltpu.VMEM((rhs, rows), jnp.float32),
            pltpu.SemaphoreType.DMA((blocks + 2,)),
        ],
        compiler_params=params,
        name="cross",
    )(*(pltpu.with_memory_space_constraint(a, pltpu.HBM) for a in operands))

    near = max(1, sections // 2 - 2)
    mask = lambda count: jax.ShapeDtypeStruct((count, quarter, variants), jnp.bfloat16)
    outside_others, outside_own, inverse, ridged = pl.pallas_call(
        functools.partial(prepare_kernel, variants * n_chrom),
        out_shape=(
            mask(near),
            mask(sections // 2),
            jax.ShapeDtypeStruct((per_device, quarter, rows), jnp.float32),
            jax.ShapeDtypeStruct((rhs, rows), jnp.float32),
        ),
        in_specs=[smem, smem, vmem],
        out_specs=(vmem,) * 4,
        compiler_params=params,
        name="prepare",
    )(widths, ridge_term, dir_t)

    def swap(x, low, high):
        return lax.ppermute(x, "samp", [(i, i ^ (high if i.bit_count() % 2 else low)) for i in range(n_samp)])

    sent = (keep_first + swap(give_first, 1, 1)).astype(jnp.bfloat16)
    mine_sum = keep_second + swap(give_second, 1, 1) + swap(sent, 3, 5)
    mine_sum, outside_others, outside_own, inverse, ridged = lax.optimization_barrier(
        (mine_sum, outside_others, outside_own, inverse, ridged)
    )
    rest = [1 << b for b in range(3, n_samp.bit_length() - 1)]
    low_bits, high_bits = rest + [4], [2] + rest
    turned = pl.pallas_call(
        turn_kernel,
        out_shape=jax.ShapeDtypeStruct((variants, rows), jnp.bfloat16),
        in_specs=[vmem],
        out_specs=vmem,
        compiler_params=params,
        name="turn",
    )(standard)
    for step, (low, high) in enumerate(zip(low_bits, high_bits)):
        mine_sum = mine_sum + swap(mine_sum.astype(jnp.bfloat16), low | 1, high | 1)
        if step == 0:
            mine_sum, turned = lax.optimization_barrier((mine_sum, turned))
    first = mine_sum.astype(jnp.bfloat16)
    second, second_sibling = swap(first, 3, 5), swap(first, 2, 4)

    def products(outside, pieces, count, dtype, name, *got):
        return pl.pallas_call(
            functools.partial(section_kernel, near if got else 0),
            out_shape=jax.ShapeDtypeStruct((count, len(pieces) * quarter, rows), dtype),
            in_specs=[vmem] * (2 + len(pieces) + len(got)),
            out_specs=vmem,
            compiler_params=params,
            cost_estimate=pl.CostEstimate(
                flops=rows * variants * half * sections, bytes_accessed=rows * variants * 2, transcendentals=0
            ),
            name=name,
        )(outside, turned, *pieces, *got)

    def swap_chrom(x, bit):
        return lax.ppermute(x, "chrom", [(i, i ^ bit) for i in range(n_chrom)])

    bit = n_chrom // 2
    for_others = lambda pieces: products(outside_others, pieces, near + 1, jnp.bfloat16, "others")
    late = (second, second_sibling)
    head = (first, swap(first, 1, 1), late[1])
    products_head = for_others(head)
    tail = (late[0],)
    gots = [swap_chrom(products_head, bit), swap_chrom(for_others(tail), bit)]
    for_own = lambda pieces, *got: products(outside_own, pieces, sections // 2, jnp.float32, "own", *got)
    if n_chrom == 2:
        own_head = for_own(head)
        own_head = pl.pallas_call(
            functools.partial(join_kernel, near),
            out_shape=jax.ShapeDtypeStruct(own_head.shape, jnp.float32),
            in_specs=[vmem] * 2,
            out_specs=vmem,
            compiler_params=params,
            name="join",
        )(own_head, gots[0])
        owns = [own_head, for_own(tail)]
    else:
        owns = [for_own(head), for_own(tail)]
        side = (lax.axis_index("chrom") // bit) % 2
        places = [received(c, sections, near, side) for c in range(sections // 2)]
        gots = [jnp.stack([lax.dynamic_index_in_dim(got, p, 0, False) for p in places]) for got in gots]
    while bit > 1:
        bit //= 2
        count = owns[0].shape[0] // 2
        side = (lax.axis_index("chrom") // bit) % 2
        sums = [own + got for own, got in zip(owns, gots)]
        gots = [
            swap_chrom(lax.dynamic_slice_in_dim(s, (1 - side) * count, count, 0).astype(jnp.bfloat16), bit) for s in sums
        ]
        owns = [lax.dynamic_slice_in_dim(s, side * count, count, 0) for s in sums]
    if n_chrom > 2:
        owns[0] = owns[0] + gots[0]

    out = pl.pallas_call(
        functools.partial(finish_kernel, near if n_chrom == 2 else 0),
        out_shape=jax.ShapeDtypeStruct((per_device, rhs, rows), jnp.float32),
        in_specs=[vmem] * 5,
        out_specs=vmem,
        compiler_params=params,
        name="finish",
    )(inverse, ridged, *owns, gots[1])
    return jnp.transpose(out, (0, 2, 1))


def solution(mesh):
    return jax.shard_map(
        on_device,
        mesh=mesh,
        in_specs=(P("samp", "chrom"), P("chrom"), P(), P(), P("samp", None)),
        out_specs=P("chrom", "samp", None),
        check_vma=False,
    )
```

```python
import functools

import jax
import jax.numpy as jnp
from jax import lax
from jax.experimental import pallas as pl
from jax.experimental.pallas import tpu as pltpu
from jax.sharding import PartitionSpec as P

VMEM_LIMIT = 24 * 1024 * 1024
BLOCK = 512


def half_and_bits():
    samp = lax.axis_index("samp")
    half, bit = samp % 2, 2
    while bit < lax.axis_size("samp"):
        half, bit = half + (samp // bit) % 2, bit * 2
    half = half % 2
    y, z = (samp // 2) % 2, (samp // 4) % 2
    return half, jnp.where(half == 0, y, z), jnp.where(half == 0, z, y)


def piece_rows(rhs):
    which, mine, sibling = half_and_bits()
    half, quarter = rhs // 2, rhs // 4
    return [
        which * half + mine * quarter,
        (1 - which) * half + sibling * quarter,
        which * half + (1 - mine) * quarter,
        (1 - which) * half + (1 - sibling) * quarter,
    ]


def cross_kernel(blocks, geno_hbm, freq_hbm, dir_hbm, stand_ref, *refs):
    quarters, (geno, freq_ref, dir_ref, sems) = refs[:4], refs[4:]
    width = geno_hbm.shape[1] // blocks
    small = [
        pltpu.make_async_copy(freq_hbm, freq_ref, sems.at[blocks]),
        pltpu.make_async_copy(dir_hbm, dir_ref, sems.at[blocks + 1]),
    ]
    for copy in small:
        copy.start()
    copies = []
    for i in range(blocks):
        columns = pl.ds(i * width, width)
        copies.append(pltpu.make_async_copy(geno_hbm.at[:, columns], geno.at[:, columns], sems.at[i]))
        copies[-1].start()
    quarter = dir_ref.shape[0] // 4
    mine, sibling, sent, sibling_sent = piece_rows(dir_ref.shape[0])
    for copy in small:
        copy.wait()
    vector = jnp.concatenate(
        [dir_ref[pl.ds(pl.multiple_of(row, quarter), quarter), :] for row in (sibling_sent, sibling, sent, mine)], axis=0
    ).astype(jnp.bfloat16)
    for i in range(blocks):
        columns = pl.ds(i * width, width)
        doubled = 2.0 * freq_ref[:, columns]
        scale = lax.rsqrt(doubled * (1.0 - freq_ref[:, columns]))
        copies[i].wait()
        standard = ((geno[:, columns].astype(jnp.float32) - doubled) * scale).astype(jnp.bfloat16)
        stand_ref[:, columns] = standard
        crossed = jnp.dot(vector, standard, preferred_element_type=jnp.float32)
        for q, ref in enumerate(quarters):
            ref[:, columns] = crossed[q * quarter : (q + 1) * quarter].astype(ref.dtype)


def prepare_kernel(total, widths_ref, ridge_ref, dir_ref, others_ref, own_ref, inverse_ref, ridged_ref):
    sections = widths_ref.shape[0]
    _, rows, variants = own_ref.shape
    per_device = inverse_ref.shape[0]
    near = others_ref.shape[0]
    rhs = dir_ref.shape[0]
    chrom = lax.axis_index("chrom")
    side = (chrom // (lax.axis_size("chrom") // 2)) % 2
    var = chrom * variants + lax.broadcasted_iota(jnp.int32, (1, variants), 1)
    start = jnp.int32(0)
    for c in range(sections):
        end = start + widths_ref[c]
        outside = jnp.where((var < start) | (var >= end), 1.0, 0.0)
        outside = jnp.broadcast_to(outside, (rows, variants)).astype(jnp.bfloat16)
        here = side == (0 if c < sections // 2 else 1)

        @pl.when(here)
        def _():
            own_ref[c % (sections // 2)] = outside

        if sections // 2 - near <= c < sections // 2 + near:

            @pl.when(jnp.logical_not(here))
            def _():
                others_ref[c - (sections // 2 - near if c < sections // 2 else sections // 2)] = outside

        start = end
    for c in range(per_device):
        divisor = (total - widths_ref[chrom * per_device + c]).astype(jnp.float32)
        inverse_ref[c] = 1.0 / jnp.full(inverse_ref.shape[1:], divisor, jnp.float32)
    for p, row in enumerate(piece_rows(rhs)):
        quarter = rhs // 4
        ridged_ref[pl.ds(p * quarter, quarter), :] = ridge_ref[0] * dir_ref[pl.ds(pl.multiple_of(row, quarter), quarter), :]


def received(c, sections, near, side):
    if sections // 2 <= near:
        return c + 1
    low = c - (sections // 2 - near) + 1
    return jnp.where(side == 0, max(low, 0), c + 1 if c < near else 0)


def turn_kernel(stand_ref, turned_ref):
    turned_ref[...] = stand_ref[...].T


def section_kernel(near, outside_ref, turned_ref, *refs):
    pieces, got_ref, out_ref = (refs[:-2] if near else refs[:-1]), refs[-2], refs[-1]
    count = outside_ref.shape[0]
    spread = [p[...] for p in pieces] if out_ref.shape[0] > count else []
    spread += [p[...] * outside_ref[c] for c in range(count) for p in pieces]
    product = jnp.dot(jnp.concatenate(spread, axis=0), turned_ref[...], preferred_element_type=jnp.float32)
    product = product.reshape(out_ref.shape)
    if not near:
        out_ref[...] = product.astype(out_ref.dtype)
        return
    side = lax.axis_index("chrom")
    for c in range(count):
        out_ref[c] = product[c] + got_ref[received(c, 2 * count, near, side)].astype(jnp.float32)


def finish_kernel(near, group, inverse_ref, ridged_ref, own_ref, got_ref, *refs):
    out_hbm, done, sems = refs[-3:]
    per_device, rhs, _ = out_hbm.shape
    side = lax.axis_index("chrom")
    places = [received(c, 2 * per_device, near, side) if near else c for c in range(per_device)]
    quarter = rhs // 4
    own_pieces = ((0, 1, 3), (2,))[group]
    copies = []
    for p, piece in enumerate(own_pieces):
        row = piece_rows(rhs)[piece]
        here = pl.ds(p * quarter, quarter)
        ridged = ridged_ref[pl.ds(piece * quarter, quarter), :]
        for c in range(per_device):
            rest = own_ref[c, here, :] + got_ref[places[c], here, :].astype(jnp.float32)
            done[p, c] = ridged + rest * inverse_ref[c]
        to = out_hbm.at[:, pl.ds(pl.multiple_of(row, quarter), quarter), :]
        copies.append(pltpu.make_async_copy(done.at[p], to, sems.at[p]))
        copies[-1].start()
    for copy in copies:
        copy.wait()


def on_device(genotypes, frequency, widths, ridge_term, direction):
    rows, variants = genotypes.shape
    rhs = direction.shape[1]
    sections = widths.shape[0]
    n_samp, n_chrom = lax.axis_size("samp"), lax.axis_size("chrom")
    per_device = sections // n_chrom
    half, quarter = rhs // 2, rhs // 4
    vmem = pl.BlockSpec(memory_space=pltpu.VMEM)
    smem = pl.BlockSpec(memory_space=pltpu.SMEM)
    anywhere = pl.BlockSpec(memory_space=pl.ANY)
    params = pltpu.CompilerParams(vmem_limit_bytes=VMEM_LIMIT)
    dir_t = direction.T

    blocks = max(1, variants // BLOCK)
    operands = (genotypes, frequency.reshape(1, variants), dir_t)
    parts = [jax.ShapeDtypeStruct((quarter, variants), dtype) for dtype in (jnp.bfloat16, jnp.float32)]
    standard, give_first, give_second, keep_first, keep_second = pl.pallas_call(
        functools.partial(cross_kernel, blocks),
        out_shape=(
            jax.ShapeDtypeStruct((rows, variants), jnp.bfloat16),
            *(parts[i] for i in (0, 0, 1, 1)),
        ),
        in_specs=[pl.BlockSpec(memory_space=pl.ANY)] * 3,
        out_specs=(vmem,) * 5,
        scratch_shapes=[
            pltpu.VMEM((rows, variants), jnp.int32),
            pltpu.VMEM((1, variants), jnp.float32),
            pltpu.VMEM((rhs, rows), jnp.float32),
            pltpu.SemaphoreType.DMA((blocks + 2,)),
        ],
        compiler_params=params,
        name="cross",
    )(*(pltpu.with_memory_space_constraint(a, pltpu.HBM) for a in operands))

    near = max(1, sections // 2 - 2)
    mask = lambda count: jax.ShapeDtypeStruct((count, quarter, variants), jnp.bfloat16)
    outside_others, outside_own, inverse, ridged = pl.pallas_call(
        functools.partial(prepare_kernel, variants * n_chrom),
        out_shape=(
            mask(near),
            mask(sections // 2),
            jax.ShapeDtypeStruct((per_device, quarter, rows), jnp.float32),
            jax.ShapeDtypeStruct((rhs, rows), jnp.float32),
        ),
        in_specs=[smem, smem, vmem],
        out_specs=(vmem,) * 4,
        compiler_params=params,
        name="prepare",
    )(widths, ridge_term, dir_t)

    def swap(x, low, high):
        return lax.ppermute(x, "samp", [(i, i ^ (high if i.bit_count() % 2 else low)) for i in range(n_samp)])

    sent = (keep_first + swap(give_first, 1, 1)).astype(jnp.bfloat16)
    mine_sum = keep_second + swap(give_second, 1, 1) + swap(sent, 3, 5)
    mine_sum, outside_others, outside_own, inverse, ridged = lax.optimization_barrier(
        (mine_sum, outside_others, outside_own, inverse, ridged)
    )
    rest = [1 << b for b in range(3, n_samp.bit_length() - 1)]
    low_bits, high_bits = rest + [4], [2] + rest
    turned = pl.pallas_call(
        turn_kernel,
        out_shape=jax.ShapeDtypeStruct((variants, rows), jnp.bfloat16),
        in_specs=[vmem],
        out_specs=vmem,
        compiler_params=params,
        name="turn",
    )(standard)
    for step, (low, high) in enumerate(zip(low_bits, high_bits)):
        mine_sum = mine_sum + swap(mine_sum.astype(jnp.bfloat16), low | 1, high | 1)
        if step == 0:
            mine_sum, turned = lax.optimization_barrier((mine_sum, turned))
    first = mine_sum.astype(jnp.bfloat16)
    second, second_sibling = swap(first, 3, 5), swap(first, 2, 4)

    def products(outside, pieces, count, dtype, name, *got):
        return pl.pallas_call(
            functools.partial(section_kernel, near if got else 0),
            out_shape=jax.ShapeDtypeStruct((count, len(pieces) * quarter, rows), dtype),
            in_specs=[vmem] * (2 + len(pieces) + len(got)),
            out_specs=vmem,
            compiler_params=params,
            cost_estimate=pl.CostEstimate(
                flops=rows * variants * half * sections, bytes_accessed=rows * variants * 2, transcendentals=0
            ),
            name=name,
        )(outside, turned, *pieces, *got)

    def swap_chrom(x, bit):
        return lax.ppermute(x, "chrom", [(i, i ^ bit) for i in range(n_chrom)])

    bit = n_chrom // 2
    for_others = lambda pieces: products(outside_others, pieces, near + 1, jnp.bfloat16, "others")
    late = (second, second_sibling)
    head = (first, swap(first, 1, 1), late[1])
    products_head = for_others(head)
    tail = (late[0],)
    gots = [swap_chrom(products_head, bit), swap_chrom(for_others(tail), bit)]
    for_own = lambda pieces, *got: products(outside_own, pieces, sections // 2, jnp.float32, "own", *got)
    owns = [for_own(head), for_own(tail)]
    if bit > 1:
        side = (lax.axis_index("chrom") // bit) % 2
        places = [received(c, sections, near, side) for c in range(sections // 2)]
        gots = [jnp.stack([lax.dynamic_index_in_dim(got, p, 0, False) for p in places]) for got in gots]
    while bit > 1:
        bit //= 2
        count = owns[0].shape[0] // 2
        side = (lax.axis_index("chrom") // bit) % 2
        sums = [own + got for own, got in zip(owns, gots)]
        gots = [
            swap_chrom(lax.dynamic_slice_in_dim(s, (1 - side) * count, count, 0).astype(jnp.bfloat16), bit) for s in sums
        ]
        owns = [lax.dynamic_slice_in_dim(s, side * count, count, 0) for s in sums]

    def finish(group, *operands):
        return pl.pallas_call(
            functools.partial(finish_kernel, near if n_chrom == 2 else 0, group),
            out_shape=jax.ShapeDtypeStruct((per_device, rhs, rows), jnp.float32),
            in_specs=[vmem] * 4 + [anywhere] * group,
            out_specs=anywhere,
            scratch_shapes=[
                pltpu.VMEM((3 - 2 * group, per_device, quarter, rows), jnp.float32),
                pltpu.SemaphoreType.DMA((3 - 2 * group,)),
            ],
            input_output_aliases={4: 0} if group else {},
            compiler_params=params,
            name="finish",
        )(inverse, ridged, *operands)

    out = pltpu.with_memory_space_constraint(finish(0, owns[0], gots[0]), pltpu.HBM)
    out = finish(1, owns[1], gots[1], out)
    return jnp.transpose(out, (0, 2, 1))


def solution(mesh):
    return jax.shard_map(
        on_device,
        mesh=mesh,
        in_specs=(P("samp", "chrom"), P("chrom"), P(), P(), P("samp", None)),
        out_specs=P("chrom", "samp", None),
        check_vma=False,
    )
```

```python
import functools

import jax
import jax.numpy as jnp
from jax import lax
from jax.experimental import pallas as pl
from jax.experimental.pallas import tpu as pltpu
from jax.sharding import PartitionSpec as P

VMEM_LIMIT = 24 * 1024 * 1024
BLOCK = 768


def half_and_bits():
    samp = lax.axis_index("samp")
    half, bit = samp % 2, 2
    while bit < lax.axis_size("samp"):
        half, bit = half + (samp // bit) % 2, bit * 2
    half = half % 2
    y, z = (samp // 2) % 2, (samp // 4) % 2
    return half, jnp.where(half == 0, y, z), jnp.where(half == 0, z, y)


def piece_rows(rhs):
    which, mine, sibling = half_and_bits()
    half, quarter = rhs // 2, rhs // 4
    return [
        which * half + mine * quarter,
        (1 - which) * half + sibling * quarter,
        which * half + (1 - mine) * quarter,
        (1 - which) * half + (1 - sibling) * quarter,
    ]


def cross_kernel(blocks, geno_hbm, freq_hbm, dir_hbm, stand_ref, *refs):
    quarters, (geno, freq_ref, dir_ref, sems) = refs[:4], refs[4:]
    width = geno_hbm.shape[1] // blocks
    small = [
        pltpu.make_async_copy(freq_hbm, freq_ref, sems.at[blocks]),
        pltpu.make_async_copy(dir_hbm, dir_ref, sems.at[blocks + 1]),
    ]
    for copy in small:
        copy.start()
    copies = []
    for i in range(blocks):
        columns = pl.ds(i * width, width)
        copies.append(pltpu.make_async_copy(geno_hbm.at[:, columns], geno.at[:, columns], sems.at[i]))
        copies[-1].start()
    quarter = dir_ref.shape[0] // 4
    mine, sibling, sent, sibling_sent = piece_rows(dir_ref.shape[0])
    for copy in small:
        copy.wait()
    vector = jnp.concatenate(
        [dir_ref[pl.ds(pl.multiple_of(row, quarter), quarter), :] for row in (sibling_sent, sibling, sent, mine)], axis=0
    ).astype(jnp.bfloat16)
    for i in range(blocks):
        columns = pl.ds(i * width, width)
        doubled = 2.0 * freq_ref[:, columns]
        scale = lax.rsqrt(doubled * (1.0 - freq_ref[:, columns]))
        copies[i].wait()
        standard = ((geno[:, columns].astype(jnp.float32) - doubled) * scale).astype(jnp.bfloat16)
        stand_ref[:, columns] = standard
        crossed = jnp.dot(vector, standard, preferred_element_type=jnp.float32)
        for q, ref in enumerate(quarters):
            ref[:, columns] = crossed[q * quarter : (q + 1) * quarter].astype(ref.dtype)


def prepare_kernel(total, widths_ref, ridge_ref, dir_ref, others_ref, own_ref, inverse_ref, ridged_ref):
    sections = widths_ref.shape[0]
    _, rows, variants = own_ref.shape
    per_device = inverse_ref.shape[0]
    near = others_ref.shape[0]
    rhs = dir_ref.shape[0]
    chrom = lax.axis_index("chrom")
    side = (chrom // (lax.axis_size("chrom") // 2)) % 2
    var = chrom * variants + lax.broadcasted_iota(jnp.int32, (1, variants), 1)
    start = jnp.int32(0)
    for c in range(sections):
        end = start + widths_ref[c]
        outside = jnp.where((var < start) | (var >= end), 1.0, 0.0)
        outside = jnp.broadcast_to(outside, (rows, variants)).astype(jnp.bfloat16)
        here = side == (0 if c < sections // 2 else 1)

        @pl.when(here)
        def _():
            own_ref[c % (sections // 2)] = outside

        if sections // 2 - near <= c < sections // 2 + near:

            @pl.when(jnp.logical_not(here))
            def _():
                others_ref[c - (sections // 2 - near if c < sections // 2 else sections // 2)] = outside

        start = end
    for c in range(per_device):
        divisor = (total - widths_ref[chrom * per_device + c]).astype(jnp.float32)
        inverse_ref[c] = 1.0 / jnp.full(inverse_ref.shape[1:], divisor, jnp.float32)
    for p, row in enumerate(piece_rows(rhs)):
        quarter = rhs // 4
        ridged_ref[pl.ds(p * quarter, quarter), :] = ridge_ref[0] * dir_ref[pl.ds(pl.multiple_of(row, quarter), quarter), :]


def received(c, sections, near, side):
    if sections // 2 <= near:
        return c + 1
    low = c - (sections // 2 - near) + 1
    return jnp.where(side == 0, max(low, 0), c + 1 if c < near else 0)


def turn_kernel(stand_ref, turned_ref):
    turned_ref[...] = stand_ref[...].T


def section_kernel(near, outside_ref, turned_ref, *refs):
    pieces, got_ref, out_ref = (refs[:-2] if near else refs[:-1]), refs[-2], refs[-1]
    count = outside_ref.shape[0]
    spread = [p[...] for p in pieces] if out_ref.shape[0] > count else []
    spread += [p[...] * outside_ref[c] for c in range(count) for p in pieces]
    product = jnp.dot(jnp.concatenate(spread, axis=0), turned_ref[...], preferred_element_type=jnp.float32)
    product = product.reshape(out_ref.shape)
    if not near:
        out_ref[...] = product.astype(out_ref.dtype)
        return
    side = lax.axis_index("chrom")
    for c in range(count):
        out_ref[c] = product[c] + got_ref[received(c, 2 * count, near, side)].astype(jnp.float32)


def finish_kernel(near, group, inverse_ref, ridged_ref, own_ref, got_ref, *refs):
    out_hbm, done, sems = refs[-3:]
    per_device, rhs, _ = out_hbm.shape
    side = lax.axis_index("chrom")
    places = [received(c, 2 * per_device, near, side) if near else c for c in range(per_device)]
    quarter = rhs // 4
    own_pieces = ((0, 1, 3), (2,))[group]
    copies = []
    for p, piece in enumerate(own_pieces):
        row = piece_rows(rhs)[piece]
        here = pl.ds(p * quarter, quarter)
        ridged = ridged_ref[pl.ds(piece * quarter, quarter), :]
        for c in range(per_device):
            rest = own_ref[c, here, :] + got_ref[places[c], here, :].astype(jnp.float32)
            done[p, c] = ridged + rest * inverse_ref[c]
        to = out_hbm.at[:, pl.ds(pl.multiple_of(row, quarter), quarter), :]
        copies.append(pltpu.make_async_copy(done.at[p], to, sems.at[p]))
        copies[-1].start()
    for copy in copies:
        copy.wait()


def on_device(genotypes, frequency, widths, ridge_term, direction):
    rows, variants = genotypes.shape
    rhs = direction.shape[1]
    sections = widths.shape[0]
    n_samp, n_chrom = lax.axis_size("samp"), lax.axis_size("chrom")
    per_device = sections // n_chrom
    half, quarter = rhs // 2, rhs // 4
    vmem = pl.BlockSpec(memory_space=pltpu.VMEM)
    smem = pl.BlockSpec(memory_space=pltpu.SMEM)
    anywhere = pl.BlockSpec(memory_space=pl.ANY)
    params = pltpu.CompilerParams(vmem_limit_bytes=VMEM_LIMIT)
    dir_t = direction.T

    blocks = max(1, variants // BLOCK)
    operands = (genotypes, frequency.reshape(1, variants), dir_t)
    parts = [jax.ShapeDtypeStruct((quarter, variants), dtype) for dtype in (jnp.bfloat16, jnp.float32)]
    standard, give_first, give_second, keep_first, keep_second = pl.pallas_call(
        functools.partial(cross_kernel, blocks),
        out_shape=(
            jax.ShapeDtypeStruct((rows, variants), jnp.bfloat16),
            *(parts[i] for i in (0, 0, 1, 1)),
        ),
        in_specs=[pl.BlockSpec(memory_space=pl.ANY)] * 3,
        out_specs=(vmem,) * 5,
        scratch_shapes=[
            pltpu.VMEM((rows, variants), jnp.int32),
            pltpu.VMEM((1, variants), jnp.float32),
            pltpu.VMEM((rhs, rows), jnp.float32),
            pltpu.SemaphoreType.DMA((blocks + 2,)),
        ],
        compiler_params=params,
        name="cross",
    )(*(pltpu.with_memory_space_constraint(a, pltpu.HBM) for a in operands))

    near = max(1, sections // 2 - 2)
    mask = lambda count: jax.ShapeDtypeStruct((count, quarter, variants), jnp.bfloat16)
    outside_others, outside_own, inverse, ridged = pl.pallas_call(
        functools.partial(prepare_kernel, variants * n_chrom),
        out_shape=(
            mask(near),
            mask(sections // 2),
            jax.ShapeDtypeStruct((per_device, quarter, rows), jnp.float32),
            jax.ShapeDtypeStruct((rhs, rows), jnp.float32),
        ),
        in_specs=[smem, smem, vmem],
        out_specs=(vmem,) * 4,
        compiler_params=params,
        name="prepare",
    )(widths, ridge_term, dir_t)

    def swap(x, low, high):
        return lax.ppermute(x, "samp", [(i, i ^ (high if i.bit_count() % 2 else low)) for i in range(n_samp)])

    sent = (keep_first + swap(give_first, 1, 1)).astype(jnp.bfloat16)
    mine_sum = keep_second + swap(give_second, 1, 1) + swap(sent, 3, 5)
    mine_sum, outside_others, outside_own, inverse, ridged = lax.optimization_barrier(
        (mine_sum, outside_others, outside_own, inverse, ridged)
    )
    rest = [1 << b for b in range(3, n_samp.bit_length() - 1)]
    low_bits, high_bits = rest + [4], [2] + rest
    turned = pl.pallas_call(
        turn_kernel,
        out_shape=jax.ShapeDtypeStruct((variants, rows), jnp.bfloat16),
        in_specs=[vmem],
        out_specs=vmem,
        compiler_params=params,
        name="turn",
    )(standard)
    for step, (low, high) in enumerate(zip(low_bits, high_bits)):
        mine_sum = mine_sum + swap(mine_sum.astype(jnp.bfloat16), low | 1, high | 1)
        if step == 0:
            mine_sum, turned = lax.optimization_barrier((mine_sum, turned))
    first = mine_sum.astype(jnp.bfloat16)
    second, second_sibling = swap(first, 3, 5), swap(first, 2, 4)

    def products(outside, pieces, count, dtype, name, *got):
        return pl.pallas_call(
            functools.partial(section_kernel, near if got else 0),
            out_shape=jax.ShapeDtypeStruct((count, len(pieces) * quarter, rows), dtype),
            in_specs=[vmem] * (2 + len(pieces) + len(got)),
            out_specs=vmem,
            compiler_params=params,
            cost_estimate=pl.CostEstimate(
                flops=rows * variants * half * sections, bytes_accessed=rows * variants * 2, transcendentals=0
            ),
            name=name,
        )(outside, turned, *pieces, *got)

    def swap_chrom(x, bit):
        return lax.ppermute(x, "chrom", [(i, i ^ bit) for i in range(n_chrom)])

    bit = n_chrom // 2
    for_others = lambda pieces: products(outside_others, pieces, near + 1, jnp.bfloat16, "others")
    late = (second, second_sibling)
    head = (first, swap(first, 1, 1), late[1])
    products_head = for_others(head)
    tail = (late[0],)
    gots = [swap_chrom(products_head, bit), swap_chrom(for_others(tail), bit)]
    for_own = lambda pieces, *got: products(outside_own, pieces, sections // 2, jnp.float32, "own", *got)
    owns = [for_own(head), for_own(tail)]
    if bit > 1:
        side = (lax.axis_index("chrom") // bit) % 2
        places = [received(c, sections, near, side) for c in range(sections // 2)]
        gots = [jnp.stack([lax.dynamic_index_in_dim(got, p, 0, False) for p in places]) for got in gots]
    while bit > 1:
        bit //= 2
        count = owns[0].shape[0] // 2
        side = (lax.axis_index("chrom") // bit) % 2
        sums = [own + got for own, got in zip(owns, gots)]
        gots = [
            swap_chrom(lax.dynamic_slice_in_dim(s, (1 - side) * count, count, 0).astype(jnp.bfloat16), bit) for s in sums
        ]
        owns = [lax.dynamic_slice_in_dim(s, side * count, count, 0) for s in sums]

    def finish(group, *operands):
        return pl.pallas_call(
            functools.partial(finish_kernel, near if n_chrom == 2 else 0, group),
            out_shape=jax.ShapeDtypeStruct((per_device, rhs, rows), jnp.float32),
            in_specs=[vmem] * 4 + [anywhere] * group,
            out_specs=anywhere,
            scratch_shapes=[
                pltpu.VMEM((3 - 2 * group, per_device, quarter, rows), jnp.float32),
                pltpu.SemaphoreType.DMA((3 - 2 * group,)),
            ],
            input_output_aliases={4: 0} if group else {},
            compiler_params=params,
            name="finish",
        )(inverse, ridged, *operands)

    out = pltpu.with_memory_space_constraint(finish(0, owns[0], gots[0]), pltpu.HBM)
    out = finish(1, owns[1], gots[1], out)
    return jnp.transpose(out, (0, 2, 1))


def solution(mesh):
    return jax.shard_map(
        on_device,
        mesh=mesh,
        in_specs=(P("samp", "chrom"), P("chrom"), P(), P(), P("samp", None)),
        out_specs=P("chrom", "samp", None),
        check_vma=False,
    )
```
